32 devices in a mesh: pipe: 4 (over y, core), tensor: 4 (over z), dp: 2 (over x).
Axes of the slice: x: 2, y: 2, z: 4, core: 2. Of those that a mesh axis runs over, the one named last changes fastest.
Arguments:
- narrowing_projection_weights: bfloat16 [4, 4, 5120, 256], P('pipe', None, 'tensor'), may hold values from -0.078125 to 0.078125
- widening_projection_weights: bfloat16 [4, 4, 256, 5120], P('pipe', None, None, 'tensor'), may hold values from -0.375 to 0.375
- scaling_multipliers: float32 [4, 4, 5120], P('pipe', None, 'tensor'), may hold values from 0.5 to 1.5
- slot_entry_activation: bfloat16 [4, 4, 64, 5120], P('pipe', None, 'dp', 'tensor'), may hold values from -15 to 15
- retained_section_entries: bfloat16 [2, 4, 4, 64, 5120], P(None, 'pipe', None, 'dp', 'tensor'), may hold values from -15 to 15
- slot_result_sensitivity: bfloat16 [4, 4, 64, 5120], P('pipe', None, 'dp', 'tensor'), may hold values from -4 to 4
- fresh_micro_batches: bfloat16 [1, 2, 64, 5120], P(None, None, 'dp', 'tensor'), may hold values from -15 to 15
- latest_result_sensitivity: bfloat16 [1, 2, 64, 5120], P(None, None, 'dp', 'tensor'), may hold values from -4 to 4
Outputs:
- section_outputs: bfloat16 [4, 4, 64, 5120], P('pipe', None, 'dp', 'tensor')
- input_grads: bfloat16 [4, 4, 64, 5120], P('pipe', None, 'dp', 'tensor')
- grad_down: float32 [4, 2, 5120, 256], P('pipe', None, ('tensor', 'dp'))
- grad_up: float32 [4, 2, 256, 5120], P('pipe', None, 'dp', 'tensor')
The draws below stay inside these ranges and needn't reach their ends.
All inputs are finite; a program needn't handle non-finite values.
Results may differ from the reference program's by a relative error of at most 0.025.
Values may be sent and summed in bfloat16 or wider, within the bound.
No kernel may reach another device: no remote copies, remote signals or barrier semaphores. Data moves between devices by JAX's collectives and lax.ppermute only.
A program may use at most 64 MiB of HBM per device.

```python
import math
import jax
import jax.numpy as jnp
from jax import lax

D = 5120
R = 256
TOK = 32
TICKS = 2
SECTIONS = 8
ROWS = 64
N_PIPE = 4
N_DP = 2


def scaled_field(key, shape):
    base_key, row_key, col_key = jax.random.split(key, 3)
    base_draw = jax.random.truncated_normal(base_key, -3.0, 3.0, shape, jnp.float32)
    row_scale = jnp.exp(jax.random.uniform(row_key, shape[:-1] + (1,), jnp.float32, math.log(0.2), math.log(2.0)))
    col_scale = jnp.exp(jax.random.uniform(col_key, (shape[-1],), jnp.float32, math.log(0.7), math.log(1.4)))
    position = (jnp.arange(shape[-1], dtype=jnp.float32) + 0.5) / shape[-1] - 0.5
    ramp_scale = jnp.exp(math.log(3.0) * position)
    return (base_draw * row_scale * col_scale * ramp_scale).astype(jnp.bfloat16)


def draw_slot_entry_activation(key, part):
    return scaled_field(jax.random.fold_in(key, 11), (SECTIONS // 2, 4, ROWS, D))


def draw_retained_section_entries(key, part):
    return scaled_field(jax.random.fold_in(key, 12), (TICKS, SECTIONS // 2, 4, ROWS, D))


def draw_fresh_micro_batches(key, part):
    return scaled_field(jax.random.fold_in(key, 13), (TICKS - 1, 2, ROWS, D))


def block_scale(key, dims, shards, low, top_value):
    def one(dim, shards_of):
        steps = jax.random.uniform(jax.random.fold_in(jax.random.fold_in(key, 6), dim), (shards_of,), jnp.float32, low / len(shards), top_value / len(shards))
        return jnp.repeat(jnp.exp(steps), dims[dim] // shards_of).reshape((-1,) + (1,) * (len(dims) - dim - 1))

    level = one(*shards[0])
    for cut in shards[1:]:
        level = level * one(*cut)
    return level


def bell_draw(stream_key, extent, deviation, most, pieces=(), held_as=jnp.bfloat16):
    factor_of = block_scale(stream_key, extent, pieces, -0.22, 0.18) if pieces else 1.0
    array = jax.random.normal(stream_key, extent, jnp.float32) * deviation * factor_of
    return jnp.minimum(jnp.maximum(array, -most), most).astype(held_as)


def setup_inputs(seed: int = 0) -> dict:
    keys = jax.random.split(jax.random.key(seed), 9)
    narrowing_projection_weights = bell_draw(keys[0], (SECTIONS // 2, 4, D, R), D ** -0.5, 0.078125, ((0, 4), (2, 4)))
    widening_projection_weights = bell_draw(keys[1], (SECTIONS // 2, 4, R, D), R ** -0.5, 0.375, ((0, 4), (3, 4)))
    scaling_multipliers = jnp.clip(1.0 + 0.1 * jax.random.normal(keys[2], (SECTIONS // 2, 4, D), jnp.float32), 0.5, 1.5)
    slot_entry_activation = draw_slot_entry_activation(jax.random.fold_in(keys[8], 71), 0)
    retained_section_entries = draw_retained_section_entries(jax.random.fold_in(keys[8], 71), 0)
    slot_result_sensitivity = bell_draw(keys[5], (SECTIONS // 2, 4, ROWS, D), 1.0, 4.0, ((0, 4), (2, 2), (3, 4)))
    fresh_micro_batches = draw_fresh_micro_batches(jax.random.fold_in(keys[8], 71), 0)
    latest_result_sensitivity = bell_draw(keys[7], (TICKS - 1, 2, ROWS, D), 1.0, 4.0, ((2, 2), (3, 4)))
    return {"narrowing_projection_weights": narrowing_projection_weights, "widening_projection_weights": widening_projection_weights, "scaling_multipliers": scaling_multipliers, "slot_entry_activation": slot_entry_activation, "retained_section_entries": retained_section_entries, "slot_result_sensitivity": slot_result_sensitivity, "fresh_micro_batches": fresh_micro_batches, "latest_result_sensitivity": latest_result_sensitivity}


eps = 1e-06

def prepare(rows, gain_row, w_down):
    widened = rows.astype(jnp.float32)
    scaled = (widened * gain_row[None, :]).astype(jnp.bfloat16)
    squares = lax.optimization_barrier(jnp.sum(widened * widened, axis=-1))
    latent = jnp.dot(scaled, w_down, preferred_element_type=jnp.float32)
    factor = 1.0 / jnp.sqrt(squares / D + eps)
    preact = latent * factor[:, None]
    active = jax.nn.silu(preact).astype(jnp.bfloat16)
    return (widened, scaled, latent, factor, preact, active)

def forward(rows, gain_row, w_down, w_up):
    widened, scaled, latent, factor, preact, active = prepare(rows, gain_row, w_down)
    return (widened + jnp.dot(active, w_up, preferred_element_type=jnp.float32)).astype(jnp.bfloat16)

def backward(rows, cotangent, gain_row, w_down, w_up):
    widened, scaled, latent, factor, preact, active = prepare(rows, gain_row, w_down)
    hidden_rank_gradient = jnp.dot(cotangent, w_up.T, preferred_element_type=jnp.float32)
    sigmoid_z = jax.nn.sigmoid(preact)
    preact_grad = hidden_rank_gradient * sigmoid_z * (1.0 + preact * (1.0 - sigmoid_z))
    latent_step = (preact_grad * factor[:, None]).astype(jnp.bfloat16)
    gradient_squares = -0.5 * factor ** 3 / D * lax.optimization_barrier(jnp.sum(preact_grad * latent, axis=-1))
    feature_grad = jnp.dot(latent_step, w_down.T, preferred_element_type=jnp.float32) * gain_row[None, :]
    rows_grad = (feature_grad + 2.0 * widened * gradient_squares[:, None] + cotangent.astype(jnp.float32)).astype(jnp.bfloat16)
    return (scaled, active, latent_step, rows_grad)

def holder_tick(operands):
    entry_activation_lines, stashed, upstream, w_down, w_up, gain_rows = operands
    result_activation_lines = jax.vmap(forward)(entry_activation_lines, gain_rows, w_down, w_up)
    rows_grad = jax.vmap(backward)(stashed, upstream, gain_rows, w_down, w_up)[3]
    return (result_activation_lines, rows_grad)

def slot_terms(rows_ticks, cot_ticks, gain_row, w_down, w_up):
    down_sum = jnp.zeros((N_DP, D, R), jnp.float32)
    up_sum = jnp.zeros((N_DP, R, D), jnp.float32)
    for tick_index in range(TICKS):
        scaled, active, latent_step, unused_grad = backward(rows_ticks[tick_index], cot_ticks[tick_index], gain_row, w_down, w_up)
        scaled_groups = scaled.reshape(N_DP, TOK, D).astype(jnp.float32)
        step_groups = latent_step.reshape(N_DP, TOK, R).astype(jnp.float32)
        active_groups = active.reshape(N_DP, TOK, R).astype(jnp.float32)
        cot_groups = cot_ticks[tick_index].reshape(N_DP, TOK, D).astype(jnp.float32)
        down_sum = down_sum + jnp.einsum('gnd,gnr->gdr', scaled_groups, step_groups)
        up_sum = up_sum + jnp.einsum('gnr,gnd->grd', active_groups, cot_groups)
    down_sum = lax.optimization_barrier(down_sum.astype(jnp.bfloat16)).astype(jnp.float32)
    up_sum = lax.optimization_barrier(up_sum.astype(jnp.bfloat16)).astype(jnp.float32)
    return (lax.optimization_barrier(jnp.sum(down_sum, axis=0)), lax.optimization_barrier(jnp.sum(up_sum, axis=0)))

def reference(narrowing_projection_weights, widening_projection_weights, scaling_multipliers, slot_entry_activation, retained_section_entries, slot_result_sensitivity, fresh_micro_batches, latest_result_sensitivity):
    entry_activation_lines = slot_entry_activation
    upstream = slot_result_sensitivity
    history = []
    result_activation_lines = slot_entry_activation
    rows_grad = slot_result_sensitivity
    for tick_index in range(TICKS):
        history.append(upstream)
        result_activation_lines, rows_grad = lax.map(holder_tick, (entry_activation_lines, retained_section_entries[tick_index], upstream, narrowing_projection_weights, widening_projection_weights, scaling_multipliers))
        if tick_index + 1 < TICKS:
            entering = fresh_micro_batches[tick_index]
            arriving = latest_result_sensitivity[tick_index]
            entry_activation_lines = jnp.stack([jnp.concatenate([entering[0][None], result_activation_lines[:-1, 0]], axis=0), jnp.concatenate([result_activation_lines[1:, 1], result_activation_lines[-1:, 0]], axis=0), jnp.concatenate([result_activation_lines[1:, 2], entering[1][None]], axis=0), jnp.concatenate([result_activation_lines[:1, 2], result_activation_lines[:-1, 3]], axis=0)], axis=1)
            upstream = jnp.stack([jnp.concatenate([rows_grad[1:, 0], rows_grad[-1:, 1]], axis=0), jnp.concatenate([arriving[0][None], rows_grad[:-1, 1]], axis=0), jnp.concatenate([rows_grad[:1, 3], rows_grad[:-1, 2]], axis=0), jnp.concatenate([rows_grad[1:, 3], arriving[1][None]], axis=0)], axis=1)
    cot_history = jnp.stack(history)

    def holder_grads(holder):
        mirror_index = (N_PIPE - 1 - holder).astype(jnp.int32)
        results_down = []
        results_up = []
        for position_index in range(2):
            pairs = ((holder, position_index), (mirror_index, position_index + 2))
            total_down = jnp.zeros((D, R), jnp.float32)
            total_up = jnp.zeros((R, D), jnp.float32)
            for owner, which in pairs:
                rows_ticks = lax.dynamic_index_in_dim(retained_section_entries, owner, 1, keepdims=False)[:, which]
                cot_ticks = lax.dynamic_index_in_dim(cot_history, owner, 1, keepdims=False)[:, which]
                gain_row = lax.dynamic_index_in_dim(scaling_multipliers, owner, 0, keepdims=False)[which]
                w_down = lax.dynamic_index_in_dim(narrowing_projection_weights, owner, 0, keepdims=False)[which]
                w_up = lax.dynamic_index_in_dim(widening_projection_weights, owner, 0, keepdims=False)[which]
                term_down, term_up = slot_terms(rows_ticks, cot_ticks, gain_row, w_down, w_up)
                total_down = total_down + term_down
                total_up = total_up + term_up
            results_down.append(total_down)
            results_up.append(total_up)
        return (jnp.stack(results_down), jnp.stack(results_up))
    grad_down, grad_up = lax.map(holder_grads, jnp.arange(N_PIPE, dtype=jnp.int32))
    return (result_activation_lines, rows_grad, grad_down, grad_up)
```

```python
import functools
import math

import jax
import jax.numpy as jnp
from jax import lax
from jax.experimental import pallas as pl
from jax.experimental.pallas import tpu as pltpu
from jax.sharding import PartitionSpec as P

D = 5120
EPS = 1e-06
LANES = 128
F32 = jnp.float32
BF16 = jnp.bfloat16

NN = (((1,), (0,)), ((), ()))
NT = (((1,), (1,)), ((), ()))
TN = (((0,), (0,)), ((), ()))


def dot(a, b, dims=NN):
    return lax.dot_general(a, b, dims, preferred_element_type=F32)


def params():
    return pltpu.CompilerParams(vmem_limit_bytes=48 * 2**20)


def on_lanes(columns, rows):
    lane = lax.broadcasted_iota(jnp.int32, (rows, LANES), 1)
    out = jnp.zeros((rows, LANES), F32)
    for index, column in enumerate(columns):
        out = jnp.where(lane == index, column, out)
    return out


def squares_of(rows):
    return jnp.sum(rows * rows, axis=-1, keepdims=True)


def whole(shape):
    return pl.BlockSpec(shape, lambda s, *_: (0,) * len(shape))


def deal(table, outs, place, chunk):
    for k, out in enumerate(outs):
        start = pl.multiple_of((place ^ k) * chunk, chunk)
        out[...] = table[pl.ds(start, chunk), :]


def first_partials_body(
    parts, chunk, info, x_ref, kept_ref, dy_ref, gain_ref, down_ref, up_ref, *rest
):
    outs, table = rest[:parts], rest[parts]
    s = pl.program_id(0)
    rows = x_ref.shape[0]
    ticks = kept_ref.shape[0]
    gain = gain_ref[...]
    streams = [x_ref[...].astype(F32)] + [kept_ref[t].astype(F32) for t in range(ticks)]
    scaled = jnp.concatenate([(v * gain).astype(BF16) for v in streams], axis=0)
    latent = dot(scaled, down_ref[...])
    grad = dot(dy_ref[...], up_ref[...], NT)
    pieces = [latent[i * rows : (i + 1) * rows] for i in range(ticks + 1)]
    pieces += [grad, on_lanes([squares_of(v) for v in streams], rows)]
    start = pl.multiple_of(s * rows, rows)
    table[pl.ds(start, rows), :] = jnp.concatenate(pieces, axis=1).astype(BF16)

    @pl.when(s == pl.num_programs(0) - 1)
    def _():
        deal(table, outs, info[0], chunk)


def first_partials(info, parts, x, kept, dy, gain, w_down, w_up):
    slots, rows, feats = x.shape
    ticks = kept.shape[0]
    rank = w_down.shape[-1]
    chunk = slots * rows // parts
    width = (ticks + 2) * rank + LANES
    per_slot = pl.BlockSpec((None, rows, feats), lambda s, *_: (s, 0, 0))
    return pl.pallas_call(
        functools.partial(first_partials_body, parts, chunk),
        grid_spec=pltpu.PrefetchScalarGridSpec(
            num_scalar_prefetch=1,
            grid=(slots,),
            in_specs=[
                per_slot,
                pl.BlockSpec((ticks, None, rows, feats), lambda s, *_: (0, s, 0, 0)),
                per_slot,
                pl.BlockSpec((None, 1, feats), lambda s, *_: (s, 0, 0)),
                pl.BlockSpec((None, feats, rank), lambda s, *_: (s, 0, 0)),
                pl.BlockSpec((None, rank, feats), lambda s, *_: (s, 0, 0)),
            ],
            out_specs=[whole((chunk, width))] * parts,
            scratch_shapes=[pltpu.VMEM((slots * rows, width), BF16)],
        ),
        out_shape=[jax.ShapeDtypeStruct((chunk, width), BF16)] * parts,
        compiler_params=params(),
        name="first_partials",
    )(info, x, kept, dy, gain, w_down, w_up)


def total(refs):
    value = refs[0][...].astype(F32)
    for ref in refs[1:]:
        value = value + ref[...].astype(F32)
    return value


def scale_of(squares):
    return 1.0 / jnp.sqrt(squares / D + EPS)


def logistic(z):
    return 1.0 / (1.0 + jnp.exp(-z))


def latent_grads(da, u, r, rank):
    z = u * r
    gate = logistic(z)
    dz = da * gate * (1.0 + z * (1.0 - gate))
    dss = (-0.5 / D) * r * r * r * jnp.sum(dz * u, axis=-1, keepdims=True)
    return dz * r, dss


def first_latents_body(parts, ticks, rank, *refs):
    ins, (out, held) = refs[:parts], refs[parts:]
    value = total(ins)
    chunk = value.shape[0]
    base = (ticks + 2) * rank
    streams = []
    for i in range(ticks + 1):
        u = value[:, i * rank : (i + 1) * rank]
        r = scale_of(value[:, base + i : base + i + 1])
        streams.append((u, r))
    da = value[:, (ticks + 1) * rank : base]
    du, dss = latent_grads(da, *streams[1], rank)
    actives = [u * r * logistic(u * r) for u, r in streams]
    tail = on_lanes([dss], chunk)
    out[...] = jnp.concatenate([actives[0], du, tail] + actives[1:], axis=1).astype(BF16)
    pieces = []
    for u, r in streams[2:]:
        pieces += [u, on_lanes([r], chunk)]
    held[...] = jnp.concatenate(pieces, axis=1)


def first_latents(parts, ticks, rank, received):
    chunk = received[0].shape[0]
    return pl.pallas_call(
        functools.partial(first_latents_body, parts, ticks, rank),
        out_shape=[
            jax.ShapeDtypeStruct((chunk, (ticks + 2) * rank + LANES), BF16),
            jax.ShapeDtypeStruct((chunk, (ticks - 1) * (rank + LANES)), F32),
        ],
        compiler_params=params(),
        name="first_latents",
    )(*received)


def later_latents_body(parts, rank, *refs):
    ins, held, out = refs[:parts], refs[parts], refs[parts + 1]
    value = total(ins)
    chunk = value.shape[0]
    z = value[:, :rank] * scale_of(value[:, 2 * rank : 2 * rank + 1])
    du, dss = latent_grads(
        value[:, rank : 2 * rank], held[:, :rank], held[:, rank : rank + 1], rank
    )
    pieces = [z * logistic(z), du, on_lanes([dss], chunk)]
    out[...] = jnp.concatenate(pieces, axis=1).astype(BF16)


def later_latents(parts, rank, received, held):
    chunk = received[0].shape[0]
    return pl.pallas_call(
        functools.partial(later_latents_body, parts, rank),
        out_shape=jax.ShapeDtypeStruct((chunk, 2 * rank + LANES), BF16),
        compiler_params=params(),
        name="later_latents",
    )(*received, held)


def gather_table(ins, table, place, chunk):
    for k, ref in enumerate(ins):
        start = pl.multiple_of((place ^ k) * chunk, chunk)
        table[pl.ds(start, chunk), :] = ref[...]


def slot_results(s, table, rank, x_ref, kept_ref, dy_ref, gain_ref, down_ref, up_ref):
    rows = x_ref.shape[0]
    own = table[pl.ds(pl.multiple_of(s * rows, rows), rows), :]
    active = own[:, :rank]
    du = own[:, rank : 2 * rank]
    dss = own[:, 2 * rank : 2 * rank + 1].astype(F32)
    y = x_ref[...].astype(F32) + dot(active, up_ref[...])
    dh = dot(du, down_ref[...], NT) * gain_ref[...]
    dh = dh + 2.0 * kept_ref[...].astype(F32) * dss + dy_ref[...].astype(F32)
    return y.astype(BF16), dh.astype(BF16), own


def middle_results_body(parts, chunk, rank, info, *refs):
    ins, refs = refs[:parts], refs[parts:]
    weights, (first, second, du_out, active_out, table) = refs[:6], refs[6:]
    s = pl.program_id(0)

    @pl.when(s == 0)
    def _():
        gather_table(ins, table, info[0], chunk)

    y, dh, own = slot_results(s, table, rank, *weights)
    du_out[...] = own[:, rank : 2 * rank]
    for t in range(active_out.shape[0]):
        base = 2 * rank + LANES + t * rank
        active_out[t] = own[:, base : base + rank]
    outer = jnp.logical_or(s == 0, s == 3).astype(jnp.int32)
    half = lax.shift_right_logical(s, 1)

    @pl.when(outer != info[1])
    def _():
        first[half] = y
        second[half + 2] = dh

    @pl.when(outer == info[1])
    def _():
        second[half] = y
        first[half + 2] = dh


def middle_results(info, parts, ticks, received, x, kept, dy, gain, w_down, w_up):
    slots, rows, feats = x.shape
    rank = w_down.shape[-1]
    chunk, width = received[0].shape
    per_slot = pl.BlockSpec((None, rows, feats), lambda s, *_: (s, 0, 0))
    return pl.pallas_call(
        functools.partial(middle_results_body, parts, chunk, rank),
        grid_spec=pltpu.PrefetchScalarGridSpec(
            num_scalar_prefetch=1,
            grid=(slots,),
            in_specs=[whole((chunk, width))] * parts
            + [
                per_slot,
                pl.BlockSpec((None, None, rows, feats), lambda s, *_: (0, s, 0, 0)),
                per_slot,
                pl.BlockSpec((None, 1, feats), lambda s, *_: (s, 0, 0)),
                pl.BlockSpec((None, feats, rank), lambda s, *_: (s, 0, 0)),
                pl.BlockSpec((None, rank, feats), lambda s, *_: (s, 0, 0)),
            ],
            out_specs=[
                whole((slots, rows, feats)),
                whole((slots, rows, feats)),
                pl.BlockSpec((None, rows, rank), lambda s, *_: (s, 0, 0)),
                pl.BlockSpec((ticks, None, rows, rank), lambda s, *_: (0, s, 0, 0)),
            ],
            scratch_shapes=[pltpu.VMEM((slots * rows, width), BF16)],
        ),
        out_shape=[
            jax.ShapeDtypeStruct((slots, rows, feats), BF16),
            jax.ShapeDtypeStruct((slots, rows, feats), BF16),
            jax.ShapeDtypeStruct((slots, rows, rank), BF16),
            jax.ShapeDtypeStruct((ticks, slots, rows, rank), BF16),
        ],
        compiler_params=params(),
        name="middle_results",
    )(info, *received, x, kept, dy, gain, w_down, w_up)


def later_partials_body(parts, chunk, info, *refs):
    xa, xb, ga, gb, own_x, own_g, fresh, arriving = (ref[...] for ref in refs[:8])
    gain_ref, down_ref, up_ref = refs[8:11]
    outs, (x_out, g_out, table) = refs[11 : 11 + parts], refs[11 + parts :]
    s = pl.program_id(0)
    rows = x_out.shape[0]
    outer = jnp.logical_or(s == 0, s == 3).astype(jnp.int32)
    even_slot = (s & 1) == 0
    edge = info[2] == 1
    xb = jnp.where(edge, jnp.where(even_slot, fresh, own_x), xb)
    gb = jnp.where(edge, jnp.where(even_slot, own_g, arriving), gb)
    x = jnp.where(outer == info[1], xa, xb)
    g = jnp.where(outer == info[1], gb, ga)
    x_out[...] = x
    g_out[...] = g
    wide = x.astype(F32)
    latent = dot((wide * gain_ref[...]).astype(BF16), down_ref[...])
    grad = dot(g, up_ref[...], NT)
    pieces = [latent, grad, on_lanes([squares_of(wide)], rows)]
    start = pl.multiple_of(s * rows, rows)
    table[pl.ds(start, rows), :] = jnp.concatenate(pieces, axis=1).astype(BF16)

    @pl.when(s == pl.num_programs(0) - 1)
    def _():
        deal(table, outs, info[0], chunk)


def later_partials(info, parts, first, second, own, fresh, arriving, gain, w_down, w_up):
    slots, rows, feats = first.shape
    rank = w_down.shape[-1]
    chunk = slots * rows // parts
    width = 2 * rank + LANES
    act = pl.BlockSpec((None, rows, feats), lambda s, *_: (s // 2, 0, 0))
    sens = pl.BlockSpec((None, rows, feats), lambda s, *_: (2 + s // 2, 0, 0))
    per_slot = pl.BlockSpec((None, rows, feats), lambda s, *_: (s, 0, 0))
    return pl.pallas_call(
        functools.partial(later_partials_body, parts, chunk),
        grid_spec=pltpu.PrefetchScalarGridSpec(
            num_scalar_prefetch=1,
            grid=(slots,),
            in_specs=[
                act,
                act,
                sens,
                sens,
                act,
                sens,
                act,
                act,
                pl.BlockSpec((None, 1, feats), lambda s, *_: (s, 0, 0)),
                pl.BlockSpec((None, feats, rank), lambda s, *_: (s, 0, 0)),
                pl.BlockSpec((None, rank, feats), lambda s, *_: (s, 0, 0)),
            ],
            out_specs=[whole((chunk, width))] * parts + [per_slot, per_slot],
            scratch_shapes=[pltpu.VMEM((slots * rows, width), BF16)],
        ),
        out_shape=[jax.ShapeDtypeStruct((chunk, width), BF16)] * parts
        + [jax.ShapeDtypeStruct((slots, rows, feats), BF16)] * 2,
        compiler_params=params(),
        name="later_partials",
    )(info, first, second, first, second, own, own, fresh, arriving, gain, w_down, w_up)


def last_results_body(parts, chunk, rank, info, *refs):
    ins, refs = refs[:parts], refs[parts:]
    weights, (y_out, dh_out, du_out, table) = refs[:6], refs[6:]
    s = pl.program_id(0)

    @pl.when(s == 0)
    def _():
        gather_table(ins, table, info[0], chunk)

    y, dh, own = slot_results(s, table, rank, *weights)
    y_out[...] = y
    dh_out[...] = dh
    du_out[...] = own[:, rank : 2 * rank]


def last_results(info, parts, tick, received, x, kept, dy, gain, w_down, w_up):
    slots, rows, feats = x.shape
    rank = w_down.shape[-1]
    chunk, width = received[0].shape
    per_slot = pl.BlockSpec((None, rows, feats), lambda s, *_: (s, 0, 0))
    return pl.pallas_call(
        functools.partial(last_results_body, parts, chunk, rank),
        grid_spec=pltpu.PrefetchScalarGridSpec(
            num_scalar_prefetch=1,
            grid=(slots,),
            in_specs=[whole((chunk, width))] * parts
            + [
                per_slot,
                pl.BlockSpec((None, None, rows, feats), lambda s, *_: (tick, s, 0, 0)),
                per_slot,
                pl.BlockSpec((None, 1, feats), lambda s, *_: (s, 0, 0)),
                pl.BlockSpec((None, feats, rank), lambda s, *_: (s, 0, 0)),
                pl.BlockSpec((None, rank, feats), lambda s, *_: (s, 0, 0)),
            ],
            out_specs=[
                per_slot,
                per_slot,
                pl.BlockSpec((None, rows, rank), lambda s, *_: (s, 0, 0)),
            ],
            scratch_shapes=[pltpu.VMEM((slots * rows, width), BF16)],
        ),
        out_shape=[
            jax.ShapeDtypeStruct((slots, rows, feats), BF16),
            jax.ShapeDtypeStruct((slots, rows, feats), BF16),
            jax.ShapeDtypeStruct((slots, rows, rank), BF16),
        ],
        compiler_params=params(),
        name="last_results",
    )(info, *received, x, kept, dy, gain, w_down, w_up)


def weight_grads(sources, ticks):
    specs, operands, layout = [], [], []
    for source in sources:
        for array in source:
            if array.ndim == 4:
                spec = pl.BlockSpec(
                    (array.shape[0], None) + array.shape[2:], lambda j: (0, j, 0, 0)
                )
            else:
                spec = pl.BlockSpec((None,) + array.shape[1:], lambda j: (j, 0, 0))
            specs.append(spec)
            operands.append(array)
    hg, dy0, act, du0, dy1, du1 = sources[0]

    def body(*refs):
        ins, (down_out, up_out) = refs[:-2], refs[-2:]
        hgs, dus, acts, dys = [], [], [], []
        for index in range(len(sources)):
            h, d0, a, l0, d1, l1 = ins[6 * index : 6 * index + 6]
            for t in range(ticks):
                hgs.append(h[t])
                acts.append(a[t])
                dus.append(l0[...] if t == 0 else l1[...])
                dys.append(d0[...] if t == 0 else d1[...])
        stack = functools.partial(jnp.concatenate, axis=0)
        down_out[...] = dot(stack(hgs), stack(dus), TN)
        up_out[...] = dot(stack(acts), stack(dys), TN)

    feats, rank = hg.shape[-1], du0.shape[-1]
    some_rank, all_feats = act.shape[-1], dy0.shape[-1]
    return pl.pallas_call(
        body,
        grid=(2,),
        in_specs=specs,
        out_specs=[
            pl.BlockSpec((None, feats, rank), lambda j: (j, 0, 0)),
            pl.BlockSpec((None, some_rank, all_feats), lambda j: (j, 0, 0)),
        ],
        out_shape=[
            jax.ShapeDtypeStruct((2, feats, rank), F32),
            jax.ShapeDtypeStruct((2, some_rank, all_feats), F32),
        ],
        compiler_params=params(),
        name="weight_grads",
    )(*operands)


def share(array, axis, count, index):
    size = array.shape[axis] // count
    return lax.dynamic_slice_in_dim(array, index * size, size, axis=axis)


def packed(arrays, width):
    pieces = []
    for array in arrays:
        for start in range(0, array.shape[-1], width):
            piece = lax.slice_in_dim(array, start, start + width, axis=array.ndim - 1)
            pieces.append(piece.reshape(-1, width))
    return jnp.concatenate(pieces, axis=0)


def unpacked(value, shapes):
    width = value.shape[-1]
    out, start = [], 0
    for shape in shapes:
        count, pieces = math.prod(shape[:-1]), []
        for _ in range(shape[-1] // width):
            pieces.append(value[start : start + count].reshape(shape[:-1] + (width,)))
            start += count
        out.append(pieces[0] if len(pieces) == 1 else jnp.concatenate(pieces, axis=-1))
    return out


def per_device(w_down, w_up, gains, entry, kept, upstream, fresh, arriving):
    holders, parts, groups = (lax.axis_size(a) for a in ("pipe", "tensor", "dp"))
    position = lax.axis_index("pipe")
    place = lax.axis_index("tensor")
    group = lax.axis_index("dp")
    w_down, w_up, gains = w_down[0], w_up[0], gains[0]
    x, kept, dy = entry[0], kept[:, 0], upstream[0]
    slots, rows, feats = x.shape
    ticks = kept.shape[0]
    rank = w_down.shape[-1]
    gain = gains[:, None, :]
    odd = position % 2
    edge = jnp.logical_or(position == 0, position == holders - 1)
    info = jnp.stack([place, odd, edge]).astype(jnp.int32)

    def around(arrays):
        return [arrays[0]] + [
            lax.ppermute(arrays[k], "tensor", [(i, i ^ k) for i in range(parts)])
            for k in range(1, parts)
        ]

    def relayed(near, far):
        out = []
        for k in range(1, groups):
            out.append(lax.ppermute(near(k), "dp", [(i, i ^ k) for i in range(groups)]))
        for k in range(groups):
            pairs = [
                (d * groups + i, (holders - 1 - d) * groups + (i ^ k))
                for d in range(holders)
                for i in range(groups)
            ]
            out.append(lax.ppermute(far(k), ("pipe", "dp"), pairs))
        return out

    dealt = first_partials(info, parts, x, kept, dy, gain, w_down, w_up)
    received = around(dealt)
    message, held = first_latents(parts, ticks, rank, received)
    received = around([message] * parts)
    first, second, du0, actives = middle_results(
        info, parts, ticks, received, x, kept, dy, gain, w_down, w_up
    )

    wide = feats // groups
    scaled = (kept.astype(F32) * gain[None]).astype(BF16)

    def early(lo):
        return lambda k: packed(
            [share(scaled[:, lo : lo + 2], 3, groups, group ^ k), dy[lo : lo + 2]], wide
        )

    early_in = relayed(early(0), early(2))

    swap = [(i, i ^ 1) for i in range(holders)]
    cross = [p for i in range(1, holders - 1, 2) for p in ((i, i + 1), (i + 1, i))]
    from_first = lax.ppermute(first, "pipe", swap)
    from_second = lax.ppermute(second, "pipe", cross) if cross else second
    *dealt, x1, g1 = later_partials(
        info, parts, from_first, from_second, second, fresh[0], arriving[0], gain, w_down, w_up
    )

    some = rank // groups

    def middle(lo):
        return lambda k: packed(
            [
                share(actives[:, lo : lo + 2], 3, groups, group ^ k),
                du0[lo : lo + 2],
                g1[lo : lo + 2],
            ],
            some,
        )

    received = around(dealt)
    middle_in = relayed(middle(0), middle(2))
    message = later_latents(parts, rank, received, held)
    received = around([message] * parts)
    y, dh, du1 = last_results(
        info, parts, ticks - 1, received, x1, kept, g1, gain, w_down, w_up
    )
    late_in = relayed(lambda k: du1[:2], lambda k: du1[2:])

    sources = [
        (
            share(scaled[:, :2], 3, groups, group),
            dy[:2],
            share(actives[:, :2], 3, groups, group),
            du0[:2],
            g1[:2],
            du1[:2],
        )
    ]
    for e, m, l in zip(early_in, middle_in, late_in):
        hg, dy0 = unpacked(e, [(ticks, 2, rows, wide), (2, rows, feats)])
        act, first_du, dy1 = unpacked(
            m, [(ticks, 2, rows, some), (2, rows, rank), (2, rows, feats)]
        )
        sources.append((hg, dy0, act, first_du, dy1, l))
    grad_down, grad_up = weight_grads(sources, ticks)
    return y[None], dh[None], grad_down[None], grad_up[None]


def solution(mesh):
    return jax.shard_map(
        per_device,
        mesh=mesh,
        in_specs=(
            P("pipe", None, "tensor", None),
            P("pipe", None, None, "tensor"),
            P("pipe", None, "tensor"),
            P("pipe", None, "dp", "tensor"),
            P(None, "pipe", None, "dp", "tensor"),
            P("pipe", None, "dp", "tensor"),
            P(None, None, "dp", "tensor"),
            P(None, None, "dp", "tensor"),
        ),
        out_specs=(
            P("pipe", None, "dp", "tensor"),
            P("pipe", None, "dp", "tensor"),
            P("pipe", None, ("tensor", "dp"), None),
            P("pipe", None, "dp", "tensor"),
        ),
        check_vma=False,
    )
```

```python
import functools

import jax
import jax.numpy as jnp
from jax import lax
from jax.experimental import pallas as pl
from jax.experimental.pallas import tpu as pltpu
from jax.sharding import PartitionSpec as P

D = 5120
EPS = 1e-06
LANES = 128
F32 = jnp.float32
BF16 = jnp.bfloat16

COSTS = {
    "first_partials": 5.0,
    "early_factors": 0.3,
    "held_weights": 0.5,
    "marker": 1.5,
    "first_latents": 0.3,
    "second_results": 0.8,
    "first_results": 0.8,
    "later_partials": 1.3,
    "middle_factors": 0.1,
    "early_share": 0.3,
    "middle_share": 0.2,
    "late_share": 0.1,
    "later_latents": 0.3,
    "late_factors": 0.2,
    "last_results": 0.7,
    "up_grads": 0.4,
    "down_grads": 1.5
}
FLOPS_PER_US = 1.1e9

NN = (((1,), (0,)), ((), ()))
NT = (((1,), (1,)), ((), ()))
TN = (((0,), (0,)), ((), ()))


def dot(a, b, dims=NN):
    return lax.dot_general(a, b, dims, preferred_element_type=F32)


def call(body, operands, outs, name, scratch=(), limit=24, after=(), raw=0):
    count = len(operands)

    def run(*refs):
        body(*refs[:count], *refs[count + len(after) :])

    return pl.pallas_call(
        run,
        in_specs=[pl.BlockSpec(memory_space=pl.ANY)] * raw
        + [pl.BlockSpec(memory_space=pltpu.VMEM)] * (count - raw)
        + [pl.BlockSpec(memory_space=pl.ANY)] * len(after),
        out_specs=[pl.BlockSpec(memory_space=pltpu.VMEM)] * len(outs),
        out_shape=[jax.ShapeDtypeStruct(shape, dtype) for shape, dtype in outs],
        scratch_shapes=list(scratch),
        compiler_params=pltpu.CompilerParams(vmem_limit_bytes=limit * 2**20),
        cost_estimate=pl.CostEstimate(
            flops=round(COSTS[name] * FLOPS_PER_US), bytes_accessed=0, transcendentals=0
        ),
        name=name,
    )(*operands, *after)


def place():
    return lax.axis_index("tensor")


def group():
    return lax.axis_index("dp")


def odd():
    return lax.rem(lax.axis_index("pipe"), 2) == 1


def even():
    return jnp.logical_not(odd())


def edge():
    position = lax.axis_index("pipe")
    return jnp.logical_or(position == 0, position == lax.axis_size("pipe") - 1)


def on_lanes(columns, rows):
    lane = lax.broadcasted_iota(jnp.int32, (rows, LANES), 1)
    out = jnp.zeros((rows, LANES), F32)
    for index, column in enumerate(columns):
        out = jnp.where(lane == index, column, out)
    return out


def squares_of(rows):
    return jnp.sum(rows * rows, axis=-1, keepdims=True)


def lane_part(value, index, count):
    size = value.shape[-1] // count
    out = value[:, :size]
    for i in range(1, count):
        out = jnp.where(index == i, value[:, i * size : (i + 1) * size], out)
    return out


def deal(table, outs):
    here, chunk = place(), outs[0].shape[0]
    for k, out in enumerate(outs):
        start = pl.multiple_of((here ^ k) * chunk, chunk)
        out[...] = table[pl.ds(start, chunk), :]


def collect(ins, table):
    here, chunk = place(), ins[0].shape[0]
    for k, ref in enumerate(ins):
        start = pl.multiple_of((here ^ k) * chunk, chunk)
        table[pl.ds(start, chunk), :] = ref[...]


def first_partials(parts, w_down, w_up, gains, entry, kept, upstream, after):
    _, slots, rows, feats = entry.shape
    ticks, rank = kept.shape[0], w_down.shape[-1]
    width = (ticks + 2) * rank + LANES

    def body(down_ref, up_ref, gain_ref, x_ref, kept_ref, dy_ref, *rest):
        outs, table = rest[:parts], rest[parts]
        for s in range(slots):
            gain = gain_ref[0, s : s + 1, :]
            here = slice(s * rows, (s + 1) * rows)
            streams = [x_ref[0, s].astype(F32)]
            streams += [kept_ref[t, 0, s].astype(F32) for t in range(ticks)]
            scaled = jnp.concatenate([(v * gain).astype(BF16) for v in streams], axis=0)
            latent = dot(scaled, down_ref[0, s]).astype(BF16)
            for i in range(ticks + 1):
                table[here, i * rank : (i + 1) * rank] = latent[i * rows : (i + 1) * rows]
            base = (ticks + 1) * rank
            table[here, base : base + rank] = dot(dy_ref[0, s], up_ref[0, s], NT).astype(BF16)
            squares = on_lanes([squares_of(v) for v in streams], rows)
            table[here, base + rank :] = squares.astype(BF16)
        deal(table, outs)

    return call(
        body,
        [w_down, w_up, gains, entry, kept, upstream],
        [((slots * rows // parts, width), BF16)] * parts,
        "first_partials",
        [pltpu.VMEM((slots * rows, width), BF16)],
        limit=62,
        after=after,
    )


def early_factors(gains, kept, upstream, own, after):
    ticks, _, slots, rows, feats = kept.shape
    half = slots // 2

    def body(gain_ref, kept_ref, dy_ref, own_ref, near, far, own_out):
        own_out[...] = own_ref[...]
        for s in range(slots):
            gain = gain_ref[0, s : s + 1, :]
            out = near if s < half else far
            for t in range(ticks):
                hg = kept_ref[t, 0, s].astype(F32) * gain
                out[s % half, :, t * feats : (t + 1) * feats] = hg.astype(BF16)
            out[s % half, :, ticks * feats :] = dy_ref[0, s]

    return call(
        body,
        [gains, kept, upstream, own],
        [((half, rows, (ticks + 1) * feats), BF16)] * 2 + [(own.shape, own.dtype)],
        "early_factors",
        after=after,
    )


def shared(name, groups, cut, near, far, after=()):
    half, rows, width = near.shape
    count = sum(size for _, size in cut)
    kept = width - count + count // groups

    def body(near_ref, far_ref, *outs):
        mine = group()
        for j in range(2 * half):
            ref = near_ref if j < half else far_ref
            for k, out in enumerate(outs):
                source, target = 0, 0
                for start, size in [*cut, (width, 0)]:
                    plain = start - source
                    if plain:
                        out[j, :, target : target + plain] = ref[j % half, :, source:start]
                    source, target = start, target + plain
                    if size:
                        run = ref[j % half, :, start : start + size].astype(F32)
                        part = lane_part(run, mine ^ k, groups).astype(BF16)
                        out[j, :, target : target + size // groups] = part
                        source, target = start + size, target + size // groups

    return call(
        body, [near, far], [((2 * half, rows, kept), BF16)] * groups, name, after=after
    )


def held_weights(w_down, w_up, after):
    def body(down_ref, up_ref, down_out, up_out, sems):
        copies = [
            pltpu.make_async_copy(down_ref, down_out, sems.at[0]),
            pltpu.make_async_copy(up_ref, up_out, sems.at[1]),
        ]
        for copy in copies:
            copy.start()
        for copy in copies:
            copy.wait()

    return call(
        body,
        [w_down, w_up],
        [(w_down.shape, w_down.dtype), (w_up.shape, w_up.dtype)],
        "held_weights",
        [pltpu.SemaphoreType.DMA((2,))],
        after=after,
        raw=2,
    )


def marker(after):
    def body(out):
        out[...] = jnp.zeros(out.shape, out.dtype)

    return call(body, [], [((8, LANES), F32)], "marker", after=after)


def total(refs):
    value = refs[0][...].astype(F32)
    for ref in refs[1:]:
        value = value + ref[...].astype(F32)
    return value


def scale_of(squares):
    return 1.0 / jnp.sqrt(squares / D + EPS)


def logistic(z):
    return 1.0 / (1.0 + jnp.exp(-z))


def latent_grads(da, u, r):
    z = u * r
    gate = logistic(z)
    dz = da * gate * (1.0 + z * (1.0 - gate))
    dss = (-0.5 / D) * r * r * r * jnp.sum(dz * u, axis=-1, keepdims=True)
    return dz * r, dss


def first_latents(ticks, rank, received, after):
    parts, chunk = len(received), received[0].shape[0]

    def body(*refs):
        ins, (out, held) = refs[:parts], refs[parts:]
        value = total(ins)
        base = (ticks + 2) * rank
        streams = []
        for i in range(ticks + 1):
            u = value[:, i * rank : (i + 1) * rank]
            streams.append((u, scale_of(value[:, base + i : base + i + 1])))
        du, dss = latent_grads(value[:, base - rank : base], *streams[1])
        active = [u * r * logistic(u * r) for u, r in streams]
        out[:, :rank] = active[0].astype(BF16)
        out[:, rank : 2 * rank] = du.astype(BF16)
        out[:, 2 * rank : 2 * rank + LANES] = on_lanes([dss], chunk).astype(BF16)
        for t in range(ticks):
            start = 2 * rank + LANES + t * rank
            out[:, start : start + rank] = active[t + 1].astype(BF16)
        u, r = streams[2]
        held[:, :rank] = u
        held[:, rank:] = on_lanes([r], chunk)

    return call(
        body,
        received,
        [((chunk, (ticks + 2) * rank + LANES), BF16), ((chunk, rank + LANES), F32)],
        "first_latents",
        after=after,
    )


def later_latents(rank, received, held, after):
    parts, chunk = len(received), received[0].shape[0]

    def body(*refs):
        ins, held, out = refs[:parts], refs[parts], refs[parts + 1]
        value = total(ins)
        z = value[:, :rank] * scale_of(value[:, 2 * rank : 2 * rank + 1])
        grads = value[:, rank : 2 * rank]
        du, dss = latent_grads(grads, held[:, :rank], held[:, rank : rank + 1])
        out[:, :rank] = (z * logistic(z)).astype(BF16)
        out[:, rank : 2 * rank] = du.astype(BF16)
        out[:, 2 * rank :] = on_lanes([dss], chunk).astype(BF16)

    outs = [((chunk, 2 * rank + LANES), BF16)]
    return call(body, [*received, held], outs, "later_latents", after=after)[0]


def slot_results(own, x, kept, dy, gain, w_down, w_up):
    rank = w_down.shape[-1]
    y = x.astype(F32) + dot(own[:, :rank], w_up)
    dss = own[:, 2 * rank : 2 * rank + 1].astype(F32)
    dh = dot(own[:, rank : 2 * rank], w_down, NT) * gain
    dh = dh + 2.0 * kept.astype(F32) * dss + dy.astype(F32)
    return y.astype(BF16), dh.astype(BF16)


def middle_results(
    name, mine, received, w_down, w_up, gains, entry, kept, upstream, factors=False, after=()
):
    parts = len(received)
    _, slots, rows, feats = entry.shape
    ticks, rank = kept.shape[0], w_down.shape[-1]
    width = received[0].shape[-1]

    def body(*refs):
        ins, refs = refs[:parts], refs[parts:]
        down_ref, up_ref, gain_ref, x_ref, kept_ref, dy_ref = refs[:6]
        out, table = refs[6], refs[-1]
        collect(ins, table)
        upward = mine()
        for i in range(slots // 2):
            outer, inner = (0, 3)[i], (1, 2)[i]
            s = jnp.where(upward, outer, inner)
            own = table[pl.ds(pl.multiple_of(s * rows, rows), rows), :rank]
            y = x_ref[0, s].astype(F32) + dot(own, up_ref[0, s])
            out[i] = y.astype(BF16)
            s = jnp.where(upward, inner, outer)
            own = table[pl.ds(pl.multiple_of(s * rows, rows), rows), rank : 2 * rank + LANES]
            dh = dot(own[:, :rank], down_ref[0, s], NT) * gain_ref[0, pl.ds(s, 1), :]
            dss = own[:, rank : rank + 1].astype(F32)
            dh = dh + 2.0 * kept_ref[0, 0, s].astype(F32) * dss + dy_ref[0, s].astype(F32)
            out[2 + i] = dh.astype(BF16)
        if factors:
            for s in range(slots):
                own = table[s * rows : (s + 1) * rows, :]
                refs[7][s, :, :rank] = own[:, rank : 2 * rank]
                refs[7][s, :, rank:] = own[:, 2 * rank + LANES :]

    outs = [((slots, rows, feats), BF16)]
    if factors:
        outs.append(((slots, rows, (ticks + 1) * rank), BF16))
    return call(
        body,
        [*received, w_down, w_up, gains, entry, kept, upstream],
        outs,
        name,
        [pltpu.VMEM((slots * rows, width), BF16)],
        after=after,
    )


def later_partials(
    parts, first, second, own, fresh, arriving, w_down, w_up, gains, after
):
    slots, rows, feats = first.shape
    rank = w_down.shape[-1]
    width = 2 * rank + LANES

    def body(*refs):
        a_ref, b_ref, own_ref, fresh_ref, arriving_ref, down_ref, up_ref, gain_ref = refs[:8]
        outs, (x_out, g_out, table) = refs[8 : 8 + parts], refs[8 + parts :]
        odd_one, at_edge = odd(), edge()
        for s in range(slots):
            i, j = s // 2, 2 + s // 2
            ends = (fresh_ref[0, i], own_ref[j]) if s % 2 == 0 else (own_ref[i], arriving_ref[0, i])
            second_x = jnp.where(at_edge, ends[0], b_ref[i])
            second_g = jnp.where(at_edge, ends[1], b_ref[j])
            outer = odd_one if s in (0, 3) else jnp.logical_not(odd_one)
            x = jnp.where(outer, a_ref[i], second_x)
            g = jnp.where(outer, second_g, a_ref[j])
            x_out[s] = x
            g_out[s] = g
            here = slice(s * rows, (s + 1) * rows)
            wide = x.astype(F32)
            scaled = (wide * gain_ref[0, s : s + 1, :]).astype(BF16)
            table[here, :rank] = dot(scaled, down_ref[0, s]).astype(BF16)
            table[here, rank : 2 * rank] = dot(g, up_ref[0, s], NT).astype(BF16)
            table[here, 2 * rank :] = on_lanes([squares_of(wide)], rows).astype(BF16)
        deal(table, outs)

    results = call(
        body,
        [first, second, own, fresh, arriving, w_down, w_up, gains],
        [((slots * rows // parts, width), BF16)] * parts
        + [((slots, rows, feats), BF16)] * 2,
        "later_partials",
        [pltpu.VMEM((slots * rows, width), BF16)],
        after=after,
    )
    return results[:parts], *results[parts:]


def middle_factors(groups, ticks, factors, g, after=()):
    slots, rows, feats = g.shape
    rank = factors.shape[-1] // (ticks + 1)
    some, half = rank // groups, slots // 2

    def body(factor_ref, g_ref, *outs):
        mine = group()
        for s in range(slots):
            for k, out in enumerate(outs[s // half * groups : (s // half + 1) * groups]):
                out[s % half, :, :feats] = g_ref[s]
                out[s % half, :, feats : feats + rank] = factor_ref[s, :, :rank]
                for t in range(ticks):
                    active = factor_ref[s, :, (t + 1) * rank : (t + 2) * rank].astype(F32)
                    part = lane_part(active, mine ^ k, groups).astype(BF16)
                    start = feats + rank + t * some
                    out[s % half, :, start : start + some] = part

    outs = call(
        body,
        [factors, g],
        [((half, rows, feats + rank + ticks * some), BF16)] * (2 * groups),
        "middle_factors",
        after=after,
    )
    return outs[:groups], outs[groups:]


def late_factors(slots, rows, rank, received, after):
    parts, (chunk, width) = len(received), received[0].shape

    def body(*refs):
        ins, (near, far, table) = refs[:parts], refs[parts:]
        here = place()
        for k, ref in enumerate(ins):
            start = pl.multiple_of((here ^ k) * chunk, chunk)
            table[pl.ds(start, chunk), :] = ref[:, rank : 2 * rank]
        for s in range(slots):
            out = near if s < slots // 2 else far
            out[s % (slots // 2)] = table[s * rows : (s + 1) * rows, :]

    return call(
        body,
        received,
        [((slots // 2, rows, rank), BF16)] * 2,
        "late_factors",
        [pltpu.VMEM((slots * rows, rank), BF16)],
        after=after,
    )


def late_share(near, far, after):
    half, rows, rank = near.shape

    def body(near_ref, far_ref, out):
        out[:half] = near_ref[...]
        out[half:] = far_ref[...]

    return call(body, [near, far], [((2 * half, rows, rank), BF16)], "late_share", after=after)[0]


def last_results(received, w_down, w_up, gains, x, kept, g):
    parts = len(received)
    slots, rows, feats = x.shape
    ticks = kept.shape[0]
    width = received[0].shape[-1]

    def body(*refs):
        ins, refs = refs[:parts], refs[parts:]
        down_ref, up_ref, gain_ref, x_ref, kept_ref, g_ref, y_out, dh_out, table = refs
        collect(ins, table)
        for s in range(slots):
            y, dh = slot_results(
                table[s * rows : (s + 1) * rows, :],
                x_ref[s],
                kept_ref[ticks - 1, 0, s],
                g_ref[s],
                gain_ref[0, s : s + 1, :],
                down_ref[0, s],
                up_ref[0, s],
            )
            y_out[0, s] = y
            dh_out[0, s] = dh

    return call(
        body,
        [*received, w_down, w_up, gains, x, kept, g],
        [((1, slots, rows, feats), BF16)] * 2,
        "last_results",
        [pltpu.VMEM((slots * rows, width), BF16)],
    )


def up_grads(groups, ticks, rank, early, mid):
    count, (slots, rows, _) = len(early), early[0].shape
    half, some = slots // 2, rank // groups
    feats = mid[0].shape[-1] - rank - ticks * some

    def body(*refs):
        early, mid, (out, token) = refs[:count], refs[count : 3 * count], refs[-2:]
        token[...] = jnp.zeros(token.shape, token.dtype)
        for j in range(half):
            act, dy = [], []
            for k, e in enumerate(early):
                for i, m in ((j, mid[k]), (half + j, mid[count + k])):
                    start = feats + rank
                    for t in range(ticks):
                        act.append(m[j, :, start + t * some : start + (t + 1) * some])
                    dy += [e[i, :, e.shape[-1] - feats :], m[j, :, :feats]]
            out[0, j] = dot(jnp.concatenate(act, axis=0), jnp.concatenate(dy, axis=0), TN)

    outs = [((1, half, some, feats), F32), ((8, LANES), F32)]
    return call(body, [*early, *mid], outs, "up_grads")


def down_grads(groups, ticks, feats, early, mid, late):
    count, (slots, rows, rank) = len(early), late[0].shape
    half, wide = slots // 2, feats // groups

    def body(*refs):
        early, mid, late = refs[:count], refs[count : 3 * count], refs[3 * count : 4 * count]
        out = refs[-1]
        for j in range(half):
            hg, du = [], []
            for k, (e, l) in enumerate(zip(early, late)):
                for i, m in ((j, mid[k]), (half + j, mid[count + k])):
                    hg += [e[i, :, t * wide : (t + 1) * wide] for t in range(ticks)]
                    du += [m[j, :, feats : feats + rank], l[i]]
            out[0, j] = dot(jnp.concatenate(hg, axis=0), jnp.concatenate(du, axis=0), TN)

    return call(
        body, [*early, *mid, *late], [((1, half, wide, rank), F32)], "down_grads"
    )[0]


def per_device(w_down, w_up, gains, entry, kept, upstream, fresh, arriving):
    holders, parts, groups = (lax.axis_size(a) for a in ("pipe", "tensor", "dp"))
    _, slots, rows, feats = entry.shape
    ticks, rank = kept.shape[0], w_down.shape[-1]

    def around(arrays):
        return [arrays[0]] + [
            lax.ppermute(arrays[k], "tensor", [(i, i ^ k) for i in range(parts)])
            for k in range(1, parts)
        ]

    def mirrored(far, k=0):
        pairs = [
            (d * groups + i, (holders - 1 - d) * groups + (i ^ k))
            for d in range(holders)
            for i in range(groups)
        ]
        return lax.ppermute(far, ("pipe", "dp"), pairs)

    def across(arrays):
        return [arrays[0]] + [
            lax.ppermute(arrays[k], "dp", [(i, i ^ k) for i in range(groups)])
            for k in range(1, groups)
        ]

    dealt = first_partials(parts, w_down, w_up, gains, entry, kept, upstream, after=[])
    received = around(dealt)

    near, far, own = early_factors(gains, kept, upstream, dealt[0], after=dealt[1:2])
    far = mirrored(far)

    weights = held_weights(w_down, w_up, after=dealt[1:2])
    message, held = first_latents(ticks, rank, [own] + received[1:], after=[near, weights[0]])
    received = around([message] * parts)

    tick = (received, *weights, gains, entry, kept, upstream)
    (second,) = middle_results("second_results", odd, *tick)
    swap = [(i, i ^ 1) for i in range(holders)]
    cross = []
    for d in range(holders):
        to = d if d in (0, holders - 1) else d + 1 if d % 2 else d - 1
        for i in range(parts):
            peer = i if to != d else i ^ (parts > 1)
            cross.append((d * parts + i, to * parts + peer))
    from_second = lax.ppermute(second, ("pipe", "tensor"), cross)
    first, factors = middle_results(
        "first_results", even, *tick, factors=True, after=[second] + []
    )
    from_first = lax.ppermute(first, "pipe", swap)

    early = across(
        shared("early_share", groups, [(t * feats, feats) for t in range(ticks)], near, far, [])
    )
    ready = marker(early[1:])

    dealt, x, g = later_partials(
        parts, from_first, from_second, second, fresh, arriving, *weights, gains, after=[]
    )
    received = around(dealt)
    near, far = middle_factors(groups, ticks, factors, g, after=[])
    mid = across(near) + [mirrored(far[k], k) for k in range(groups)]
    message = later_latents(rank, received, held, after=ready)
    received = around([message] * parts)
    grad_up, token = up_grads(groups, ticks, rank, early, mid)
    near, far = late_factors(slots, rows, rank, received, after=[])
    late = across([late_share(near, mirrored(far), after=[token])] * groups)
    y, dh = last_results(received, *weights, gains, x, kept, g)
    grad_down = down_grads(groups, ticks, feats, early, mid, late)
    return y, dh, grad_down, grad_up


def solution(mesh):
    return jax.shard_map(
        per_device,
        mesh=mesh,
        in_specs=(
            P("pipe", None, "tensor", None),
            P("pipe", None, None, "tensor"),
            P("pipe", None, "tensor"),
            P("pipe", None, "dp", "tensor"),
            P(None, "pipe", None, "dp", "tensor"),
            P("pipe", None, "dp", "tensor"),
            P(None, None, "dp", "tensor"),
            P(None, None, "dp", "tensor"),
        ),
        out_specs=(
            P("pipe", None, "dp", "tensor"),
            P("pipe", None, "dp", "tensor"),
            P("pipe", None, ("tensor", "dp"), None),
            P("pipe", None, "dp", "tensor"),
        ),
        check_vma=False,
    )
```

```python
import functools

import jax
import jax.numpy as jnp
from jax import lax
from jax.experimental import pallas as pl
from jax.experimental.pallas import tpu as pltpu
from jax.sharding import PartitionSpec as P

D = 5120
EPS = 1e-06
LANES = 128
F32 = jnp.float32
BF16 = jnp.bfloat16

COSTS = {
    "first_partials": 5.0,
    "early_factors": 0.3,
    "held_weights": 0.5,
    "marker": 1.5,
    "first_latents": 0.3,
    "second_results": 0.8,
    "first_results": 0.8,
    "later_partials": 1.3,
    "middle_factors": 0.1,
    "early_share": 0.3,
    "middle_share": 0.2,
    "late_share": 0.1,
    "later_latents": 3,
    "late_factors": 0.2,
    "last_results": 0.2,
    "up_grads": 0.4,
    "down_grads": 1.5
}
FLOPS_PER_US = 1.1e9

NN = (((1,), (0,)), ((), ()))
NT = (((1,), (1,)), ((), ()))
TN = (((0,), (0,)), ((), ()))


def dot(a, b, dims=NN):
    return lax.dot_general(a, b, dims, preferred_element_type=F32)


def call(body, operands, outs, name, scratch=(), limit=24, after=(), raw=0, sent=0):
    count = len(operands)

    def run(*refs):
        body(*refs[:count], *refs[count + len(after) :])

    return pl.pallas_call(
        run,
        in_specs=[pl.BlockSpec(memory_space=pl.ANY)] * raw
        + [pl.BlockSpec(memory_space=pltpu.VMEM)] * (count - raw)
        + [pl.BlockSpec(memory_space=pl.ANY)] * len(after),
        out_specs=[pl.BlockSpec(memory_space=pl.ANY)] * sent
        + [pl.BlockSpec(memory_space=pltpu.VMEM)] * (len(outs) - sent),
        out_shape=[jax.ShapeDtypeStruct(shape, dtype) for shape, dtype in outs],
        scratch_shapes=list(scratch),
        compiler_params=pltpu.CompilerParams(vmem_limit_bytes=limit * 2**20),
        cost_estimate=pl.CostEstimate(
            flops=round(COSTS[name] * FLOPS_PER_US), bytes_accessed=0, transcendentals=0
        ),
        name=name,
    )(*operands, *after)


def place():
    return lax.axis_index("tensor")


def group():
    return lax.axis_index("dp")


def odd():
    return lax.rem(lax.axis_index("pipe"), 2) == 1


def even():
    return jnp.logical_not(odd())


def edge():
    position = lax.axis_index("pipe")
    return jnp.logical_or(position == 0, position == lax.axis_size("pipe") - 1)


def on_lanes(columns, rows):
    lane = lax.broadcasted_iota(jnp.int32, (rows, LANES), 1)
    out = jnp.zeros((rows, LANES), F32)
    for index, column in enumerate(columns):
        out = jnp.where(lane == index, column, out)
    return out


def squares_of(rows):
    return jnp.sum(rows * rows, axis=-1, keepdims=True)


def lane_part(value, index, count):
    size = value.shape[-1] // count
    out = value[:, :size]
    for i in range(1, count):
        out = jnp.where(index == i, value[:, i * size : (i + 1) * size], out)
    return out


def deal(table, outs):
    here, chunk = place(), outs[0].shape[0]
    for k, out in enumerate(outs):
        start = pl.multiple_of((here ^ k) * chunk, chunk)
        out[...] = table[pl.ds(start, chunk), :]


def collect(ins, table):
    here, chunk = place(), ins[0].shape[0]
    for k, ref in enumerate(ins):
        start = pl.multiple_of((here ^ k) * chunk, chunk)
        table[pl.ds(start, chunk), :] = ref[...]


def first_partials(parts, w_down, w_up, gains, entry, kept, upstream, after):
    _, slots, rows, feats = entry.shape
    ticks, rank = kept.shape[0], w_down.shape[-1]
    width = (ticks + 2) * rank + LANES

    def body(down_ref, up_ref, gain_ref, x_ref, kept_ref, dy_ref, *rest):
        outs, table = rest[:parts], rest[parts]
        for s in range(slots):
            gain = gain_ref[0, s : s + 1, :]
            here = slice(s * rows, (s + 1) * rows)
            streams = [x_ref[0, s].astype(F32)]
            streams += [kept_ref[t, 0, s].astype(F32) for t in range(ticks)]
            scaled = jnp.concatenate([(v * gain).astype(BF16) for v in streams], axis=0)
            latent = dot(scaled, down_ref[0, s]).astype(BF16)
            for i in range(ticks + 1):
                table[here, i * rank : (i + 1) * rank] = latent[i * rows : (i + 1) * rows]
            base = (ticks + 1) * rank
            table[here, base : base + rank] = dot(dy_ref[0, s], up_ref[0, s], NT).astype(BF16)
            squares = on_lanes([squares_of(v) for v in streams], rows)
            table[here, base + rank :] = squares.astype(BF16)
        deal(table, outs)

    return call(
        body,
        [w_down, w_up, gains, entry, kept, upstream],
        [((slots * rows // parts, width), BF16)] * parts,
        "first_partials",
        [pltpu.VMEM((slots * rows, width), BF16)],
        limit=62,
        after=after,
    )


def early_factors(gains, kept, upstream, own, after):
    ticks, _, slots, rows, feats = kept.shape
    half = slots // 2

    def body(gain_ref, kept_ref, dy_ref, own_ref, near, far, own_out):
        own_out[...] = own_ref[...]
        for s in range(slots):
            gain = gain_ref[0, s : s + 1, :]
            out = near if s < half else far
            for t in range(ticks):
                hg = kept_ref[t, 0, s].astype(F32) * gain
                out[s % half, :, t * feats : (t + 1) * feats] = hg.astype(BF16)
            out[s % half, :, ticks * feats :] = dy_ref[0, s]

    return call(
        body,
        [gains, kept, upstream, own],
        [((half, rows, (ticks + 1) * feats), BF16)] * 2 + [(own.shape, own.dtype)],
        "early_factors",
        after=after,
    )


def shared(name, groups, cut, near, far, after=()):
    half, rows, width = near.shape
    count = sum(size for _, size in cut)
    kept = width - count + count // groups

    def body(near_ref, far_ref, *outs):
        mine = group()
        for j in range(2 * half):
            ref = near_ref if j < half else far_ref
            for k, out in enumerate(outs):
                source, target = 0, 0
                for start, size in [*cut, (width, 0)]:
                    plain = start - source
                    if plain:
                        out[j, :, target : target + plain] = ref[j % half, :, source:start]
                    source, target = start, target + plain
                    if size:
                        run = ref[j % half, :, start : start + size].astype(F32)
                        part = lane_part(run, mine ^ k, groups).astype(BF16)
                        out[j, :, target : target + size // groups] = part
                        source, target = start + size, target + size // groups

    return call(
        body, [near, far], [((2 * half, rows, kept), BF16)] * groups, name, after=after
    )


def held_weights(w_down, w_up, after):
    def body(down_ref, up_ref, down_out, up_out, sems):
        copies = [
            pltpu.make_async_copy(down_ref, down_out, sems.at[0]),
            pltpu.make_async_copy(up_ref, up_out, sems.at[1]),
        ]
        for copy in copies:
            copy.start()
        for copy in copies:
            copy.wait()

    return call(
        body,
        [w_down, w_up],
        [(w_down.shape, w_down.dtype), (w_up.shape, w_up.dtype)],
        "held_weights",
        [pltpu.SemaphoreType.DMA((2,))],
        after=after,
        raw=2,
    )


def marker(after):
    def body(out):
        out[...] = jnp.zeros(out.shape, out.dtype)

    return call(body, [], [((8, LANES), F32)], "marker", after=after)


def total(refs):
    value = refs[0][...].astype(F32)
    for ref in refs[1:]:
        value = value + ref[...].astype(F32)
    return value


def scale_of(squares):
    return 1.0 / jnp.sqrt(squares / D + EPS)


def logistic(z):
    return 1.0 / (1.0 + jnp.exp(-z))


def latent_grads(da, u, r):
    z = u * r
    gate = logistic(z)
    dz = da * gate * (1.0 + z * (1.0 - gate))
    dss = (-0.5 / D) * r * r * r * jnp.sum(dz * u, axis=-1, keepdims=True)
    return dz * r, dss


def first_latents(ticks, rank, received, after):
    parts, chunk = len(received), received[0].shape[0]

    def body(*refs):
        ins, (out, held) = refs[:parts], refs[parts:]
        value = total(ins)
        base = (ticks + 2) * rank
        streams = []
        for i in range(ticks + 1):
            u = value[:, i * rank : (i + 1) * rank]
            streams.append((u, scale_of(value[:, base + i : base + i + 1])))
        du, dss = latent_grads(value[:, base - rank : base], *streams[1])
        active = [u * r * logistic(u * r) for u, r in streams]
        out[:, :rank] = active[0].astype(BF16)
        out[:, rank : 2 * rank] = du.astype(BF16)
        out[:, 2 * rank : 2 * rank + LANES] = on_lanes([dss], chunk).astype(BF16)
        for t in range(ticks):
            start = 2 * rank + LANES + t * rank
            out[:, start : start + rank] = active[t + 1].astype(BF16)
        u, r = streams[2]
        held[:, :rank] = u
        held[:, rank:] = on_lanes([r], chunk)

    return call(
        body,
        received,
        [((chunk, (ticks + 2) * rank + LANES), BF16), ((chunk, rank + LANES), F32)],
        "first_latents",
        after=after,
    )


def later_latents(rank, received, held, after):
    parts, chunk = len(received), received[0].shape[0]

    def body(*refs):
        ins, held, out = refs[:parts], refs[parts], refs[parts + 1]
        value = total(ins)
        z = value[:, :rank] * scale_of(value[:, 2 * rank : 2 * rank + 1])
        grads = value[:, rank : 2 * rank]
        du, dss = latent_grads(grads, held[:, :rank], held[:, rank : rank + 1])
        out[:, :rank] = (z * logistic(z)).astype(BF16)
        out[:, rank : 2 * rank] = du.astype(BF16)
        out[:, 2 * rank :] = on_lanes([dss], chunk).astype(BF16)

    outs = [((chunk, 2 * rank + LANES), BF16)]
    return call(body, [*received, held], outs, "later_latents", after=after)[0]


def slot_results(own, x, kept, dy, gain, w_down, w_up):
    rank = w_down.shape[-1]
    y = x.astype(F32) + dot(own[:, :rank], w_up)
    dss = own[:, 2 * rank : 2 * rank + 1].astype(F32)
    dh = dot(own[:, rank : 2 * rank], w_down, NT) * gain
    dh = dh + 2.0 * kept.astype(F32) * dss + dy.astype(F32)
    return y.astype(BF16), dh.astype(BF16)


def middle_results(
    name, mine, received, w_down, w_up, gains, entry, kept, upstream, factors=False, after=()
):
    parts = len(received)
    _, slots, rows, feats = entry.shape
    ticks, rank = kept.shape[0], w_down.shape[-1]
    width = received[0].shape[-1]

    def body(*refs):
        ins, refs = refs[:parts], refs[parts:]
        down_ref, up_ref, gain_ref, x_ref, kept_ref, dy_ref = refs[:6]
        out, table = refs[6], refs[-1]
        collect(ins, table)
        upward = mine()
        for i in range(slots // 2):
            outer, inner = (0, 3)[i], (1, 2)[i]
            s = jnp.where(upward, outer, inner)
            own = table[pl.ds(pl.multiple_of(s * rows, rows), rows), :rank]
            y = x_ref[0, s].astype(F32) + dot(own, up_ref[0, s])
            out[i] = y.astype(BF16)
            s = jnp.where(upward, inner, outer)
            own = table[pl.ds(pl.multiple_of(s * rows, rows), rows), rank : 2 * rank + LANES]
            dh = dot(own[:, :rank], down_ref[0, s], NT) * gain_ref[0, pl.ds(s, 1), :]
            dss = own[:, rank : rank + 1].astype(F32)
            dh = dh + 2.0 * kept_ref[0, 0, s].astype(F32) * dss + dy_ref[0, s].astype(F32)
            out[2 + i] = dh.astype(BF16)
        if factors:
            for s in range(slots):
                own = table[s * rows : (s + 1) * rows, :]
                refs[7][s, :, :rank] = own[:, rank : 2 * rank]
                refs[7][s, :, rank:] = own[:, 2 * rank + LANES :]

    outs = [((slots, rows, feats), BF16)]
    if factors:
        outs.append(((slots, rows, (ticks + 1) * rank), BF16))
    return call(
        body,
        [*received, w_down, w_up, gains, entry, kept, upstream],
        outs,
        name,
        [pltpu.VMEM((slots * rows, width), BF16)],
        after=after,
    )


def later_partials(
    parts, first, second, own, fresh, arriving, w_down, w_up, gains, after
):
    slots, rows, feats = first.shape
    rank = w_down.shape[-1]
    width = 2 * rank + LANES

    def body(*refs):
        a_ref, b_ref, own_ref, fresh_ref, arriving_ref, down_ref, up_ref, gain_ref = refs[:8]
        outs, (x_out, g_out, table) = refs[8 : 8 + parts], refs[8 + parts :]
        odd_one, at_edge = odd(), edge()
        for s in range(slots):
            i, j = s // 2, 2 + s // 2
            ends = (fresh_ref[0, i], own_ref[j]) if s % 2 == 0 else (own_ref[i], arriving_ref[0, i])
            second_x = jnp.where(at_edge, ends[0], b_ref[i])
            second_g = jnp.where(at_edge, ends[1], b_ref[j])
            outer = odd_one if s in (0, 3) else jnp.logical_not(odd_one)
            x = jnp.where(outer, a_ref[i], second_x)
            g = jnp.where(outer, second_g, a_ref[j])
            x_out[s] = x
            g_out[s] = g
            here = slice(s * rows, (s + 1) * rows)
            wide = x.astype(F32)
            scaled = (wide * gain_ref[0, s : s + 1, :]).astype(BF16)
            table[here, :rank] = dot(scaled, down_ref[0, s]).astype(BF16)
            table[here, rank : 2 * rank] = dot(g, up_ref[0, s], NT).astype(BF16)
            table[here, 2 * rank :] = on_lanes([squares_of(wide)], rows).astype(BF16)
        deal(table, outs)

    results = call(
        body,
        [first, second, own, fresh, arriving, w_down, w_up, gains],
        [((slots * rows // parts, width), BF16)] * parts
        + [((slots, rows, feats), BF16)] * 2,
        "later_partials",
        [pltpu.VMEM((slots * rows, width), BF16)],
        after=after,
    )
    return results[:parts], *results[parts:]


def middle_factors(groups, ticks, factors, g, after=()):
    slots, rows, feats = g.shape
    rank = factors.shape[-1] // (ticks + 1)
    some, half = rank // groups, slots // 2

    def body(factor_ref, g_ref, *outs):
        mine = group()
        for s in range(slots):
            for k, out in enumerate(outs[s // half * groups : (s // half + 1) * groups]):
                out[s % half, :, :feats] = g_ref[s]
                out[s % half, :, feats : feats + rank] = factor_ref[s, :, :rank]
                for t in range(ticks):
                    active = factor_ref[s, :, (t + 1) * rank : (t + 2) * rank].astype(F32)
                    part = lane_part(active, mine ^ k, groups).astype(BF16)
                    start = feats + rank + t * some
                    out[s % half, :, start : start + some] = part

    outs = call(
        body,
        [factors, g],
        [((half, rows, feats + rank + ticks * some), BF16)] * (2 * groups),
        "middle_factors",
        after=after,
    )
    return outs[:groups], outs[groups:]


def late_factors(slots, rows, rank, received, after):
    parts, (chunk, width) = len(received), received[0].shape

    def body(*refs):
        ins, (near, far, table) = refs[:parts], refs[parts:]
        here = place()
        for k, ref in enumerate(ins):
            start = pl.multiple_of((here ^ k) * chunk, chunk)
            table[pl.ds(start, chunk), :] = ref[:, rank : 2 * rank]
        for s in range(slots):
            out = near if s < slots // 2 else far
            out[s % (slots // 2)] = table[s * rows : (s + 1) * rows, :]

    return call(
        body,
        received,
        [((slots // 2, rows, rank), BF16)] * 2,
        "late_factors",
        [pltpu.VMEM((slots * rows, rank), BF16)],
        after=after,
    )


def sender(sems):
    copies = []

    def send(source, target):
        copies.append(pltpu.make_async_copy(source, target, sems.at[len(copies)]))
        copies[-1].start()

    def finish():
        for copy in copies:
            copy.wait()

    return send, finish


def last_results(groups, received, w_down, w_up, gains, x, kept, g, early, mid):
    parts, count = len(received), len(early)
    slots, rows, feats = x.shape
    ticks, rank = kept.shape[0], w_down.shape[-1]
    width = received[0].shape[-1]
    half, some = slots // 2, rank // groups

    def body(*refs):
        ins, refs = refs[:parts], refs[parts:]
        down_ref, up_ref, gain_ref, x_ref, kept_ref, g_ref = refs[:6]
        early, mid, refs = refs[6 : 6 + count], refs[6 + count : 6 + 3 * count], refs[6 + 3 * count :]
        y_hbm, dh_hbm, grad_hbm, table, y_out, dh_out, grad_out, sems = refs
        send, finish = sender(sems)
        for j in range(half):
            act, dy = [], []
            for k, e in enumerate(early):
                for i, m in ((j, mid[k]), (half + j, mid[count + k])):
                    start = feats + rank
                    for t in range(ticks):
                        act.append(m[j, :, start + t * some : start + (t + 1) * some])
                    dy += [e[i, :, e.shape[-1] - feats :], m[j, :, :feats]]
            grad_out[j] = dot(jnp.concatenate(act, axis=0), jnp.concatenate(dy, axis=0), TN)
            send(grad_out.at[j], grad_hbm.at[0, j])
        collect(ins, table)
        for s in range(slots):
            y, dh = slot_results(
                table[s * rows : (s + 1) * rows, :],
                x_ref[s],
                kept_ref[ticks - 1, 0, s],
                g_ref[s],
                gain_ref[0, s : s + 1, :],
                down_ref[0, s],
                up_ref[0, s],
            )
            y_out[s] = y
            dh_out[s] = dh
            send(y_out.at[s], y_hbm.at[0, s])
            send(dh_out.at[s], dh_hbm.at[0, s])
        finish()

    return call(
        body,
        [*received, w_down, w_up, gains, x, kept, g, *early, *mid],
        [((1, slots, rows, feats), BF16)] * 2 + [((1, half, some, feats), F32)],
        "last_results",
        [
            pltpu.VMEM((slots * rows, width), BF16),
            pltpu.VMEM((slots, rows, feats), BF16),
            pltpu.VMEM((slots, rows, feats), BF16),
            pltpu.VMEM((half, some, feats), F32),
            pltpu.SemaphoreType.DMA((half + 2 * slots,)),
        ],
        sent=3,
    )


def down_grads(groups, ticks, feats, early, mid, late):
    count, (half, rows, rank) = len(early), late[0].shape
    wide = feats // groups

    def body(*refs):
        early, mid, late = refs[:count], refs[count : 3 * count], refs[3 * count : 5 * count]
        grad_hbm, grad_out, sems = refs[5 * count :]
        send, finish = sender(sems)
        for j in range(half):
            hg, du = [], []
            for k, e in enumerate(early):
                for i, n in ((j, k), (half + j, count + k)):
                    hg += [e[i, :, t * wide : (t + 1) * wide] for t in range(ticks)]
                    du += [mid[n][j, :, feats : feats + rank], late[n][j]]
            grad_out[j] = dot(jnp.concatenate(hg, axis=0), jnp.concatenate(du, axis=0), TN)
            send(grad_out.at[j], grad_hbm.at[0, j])
        finish()

    return call(
        body,
        [*early, *mid, *late],
        [((1, half, wide, rank), F32)],
        "down_grads",
        [pltpu.VMEM((half, wide, rank), F32), pltpu.SemaphoreType.DMA((half,))],
        sent=1,
    )[0]


def per_device(w_down, w_up, gains, entry, kept, upstream, fresh, arriving):
    holders, parts, groups = (lax.axis_size(a) for a in ("pipe", "tensor", "dp"))
    _, slots, rows, feats = entry.shape
    ticks, rank = kept.shape[0], w_down.shape[-1]

    def around(arrays):
        return [arrays[0]] + [
            lax.ppermute(arrays[k], "tensor", [(i, i ^ k) for i in range(parts)])
            for k in range(1, parts)
        ]

    def mirrored(far, k=0):
        pairs = [
            (d * groups + i, (holders - 1 - d) * groups + (i ^ k))
            for d in range(holders)
            for i in range(groups)
        ]
        return lax.ppermute(far, ("pipe", "dp"), pairs)

    def across(arrays):
        return [arrays[0]] + [
            lax.ppermute(arrays[k], "dp", [(i, i ^ k) for i in range(groups)])
            for k in range(1, groups)
        ]

    dealt = first_partials(parts, w_down, w_up, gains, entry, kept, upstream, after=[])
    received = around(dealt)

    near, far, own = early_factors(gains, kept, upstream, dealt[0], after=dealt[1:2])
    far = mirrored(far)

    weights = held_weights(w_down, w_up, after=dealt[1:2])
    message, held = first_latents(ticks, rank, [own] + received[1:], after=[near, weights[0]])
    received = around([message] * parts)

    tick = (received, *weights, gains, entry, kept, upstream)
    (second,) = middle_results("second_results", odd, *tick)
    swap = [(i, i ^ 1) for i in range(holders)]
    cross = []
    for d in range(holders):
        to = d if d in (0, holders - 1) else d + 1 if d % 2 else d - 1
        for i in range(parts):
            peer = i if to != d else i ^ (parts > 1)
            cross.append((d * parts + i, to * parts + peer))
    from_second = lax.ppermute(second, ("pipe", "tensor"), cross)
    first, factors = middle_results(
        "first_results", even, *tick, factors=True, after=[second] + []
    )
    from_first = lax.ppermute(first, "pipe", swap)

    early = across(
        shared("early_share", groups, [(t * feats, feats) for t in range(ticks)], near, far, [])
    )
    ready = marker(early[1:])

    dealt, x, g = later_partials(
        parts, from_first, from_second, second, fresh, arriving, *weights, gains, after=[]
    )
    received = around(dealt)
    near, far = middle_factors(groups, ticks, factors, g, after=[])
    mid = across(near) + [mirrored(far[k], k) for k in range(groups)]
    message = later_latents(rank, received, held, after=ready)
    received = around([message] * parts)
    near, far = late_factors(slots, rows, rank, received, after=[])
    late = across([near] * groups) + [mirrored(far, k) for k in range(groups)]
    y, dh, grad_up = last_results(
        groups, received, *weights, gains, x, kept, g, early, mid
    )
    grad_down = down_grads(groups, ticks, feats, early, mid, late)
    return y, dh, grad_down, grad_up


def solution(mesh):
    return jax.shard_map(
        per_device,
        mesh=mesh,
        in_specs=(
            P("pipe", None, "tensor", None),
            P("pipe", None, None, "tensor"),
            P("pipe", None, "tensor"),
            P("pipe", None, "dp", "tensor"),
            P(None, "pipe", None, "dp", "tensor"),
            P("pipe", None, "dp", "tensor"),
            P(None, None, "dp", "tensor"),
            P(None, None, "dp", "tensor"),
        ),
        out_specs=(
            P("pipe", None, "dp", "tensor"),
            P("pipe", None, "dp", "tensor"),
            P("pipe", None, ("tensor", "dp"), None),
            P("pipe", None, "dp", "tensor"),
        ),
        check_vma=False,
    )
```

```python
import functools

import jax
import jax.numpy as jnp
from jax import lax
from jax.experimental import pallas as pl
from jax.experimental.pallas import tpu as pltpu
from jax.sharding import PartitionSpec as P

D = 5120
EPS = 1e-06
LANES = 128
F32 = jnp.float32
BF16 = jnp.bfloat16

COSTS = {
    "first_partials": 5.0,
    "early_factors": 0.3,
    "held_weights": 0.5,
    "marker": 1.5,
    "first_latents": 4,
    "second_results": 0.8,
    "first_results": 0.8,
    "later_partials": 1.3,
    "middle_factors": 0.1,
    "early_share": 0.3,
    "middle_share": 0.2,
    "late_share": 0.1,
    "later_latents": 3,
    "late_factors": 0.2,
    "last_results": 0.2,
    "up_grads": 0.4,
    "down_grads": 1.5
}
FLOPS_PER_US = 1.1e9

NN = (((1,), (0,)), ((), ()))
NT = (((1,), (1,)), ((), ()))
TN = (((0,), (0,)), ((), ()))


def dot(a, b, dims=NN):
    return lax.dot_general(a, b, dims, preferred_element_type=F32)


def call(body, operands, outs, name, scratch=(), limit=24, after=(), raw=0, sent=0):
    count = len(operands)

    def run(*refs):
        body(*refs[:count], *refs[count + len(after) :])

    return pl.pallas_call(
        run,
        in_specs=[pl.BlockSpec(memory_space=pl.ANY)] * raw
        + [pl.BlockSpec(memory_space=pltpu.VMEM)] * (count - raw)
        + [pl.BlockSpec(memory_space=pl.ANY)] * len(after),
        out_specs=[pl.BlockSpec(memory_space=pl.ANY)] * sent
        + [pl.BlockSpec(memory_space=pltpu.VMEM)] * (len(outs) - sent),
        out_shape=[jax.ShapeDtypeStruct(shape, dtype) for shape, dtype in outs],
        scratch_shapes=list(scratch),
        compiler_params=pltpu.CompilerParams(vmem_limit_bytes=limit * 2**20),
        cost_estimate=pl.CostEstimate(
            flops=round(COSTS[name] * FLOPS_PER_US), bytes_accessed=0, transcendentals=0
        ),
        name=name,
    )(*operands, *after)


def place():
    return lax.axis_index("tensor")


def group():
    return lax.axis_index("dp")


def odd():
    return lax.rem(lax.axis_index("pipe"), 2) == 1


def even():
    return jnp.logical_not(odd())


def edge():
    position = lax.axis_index("pipe")
    return jnp.logical_or(position == 0, position == lax.axis_size("pipe") - 1)


def on_lanes(columns, rows):
    lane = lax.broadcasted_iota(jnp.int32, (rows, LANES), 1)
    out = jnp.zeros((rows, LANES), F32)
    for index, column in enumerate(columns):
        out = jnp.where(lane == index, column, out)
    return out


def squares_of(rows):
    return jnp.sum(rows * rows, axis=-1, keepdims=True)


def lane_part(value, index, count):
    size = value.shape[-1] // count
    out = value[:, :size]
    for i in range(1, count):
        out = jnp.where(index == i, value[:, i * size : (i + 1) * size], out)
    return out


def deal(table, outs):
    here, chunk = place(), outs[0].shape[0]
    for k, out in enumerate(outs):
        start = pl.multiple_of((here ^ k) * chunk, chunk)
        out[...] = table[pl.ds(start, chunk), :]


def collect(ins, table):
    here, chunk = place(), ins[0].shape[0]
    for k, ref in enumerate(ins):
        start = pl.multiple_of((here ^ k) * chunk, chunk)
        table[pl.ds(start, chunk), :] = ref[...]


def first_partials(parts, w_down, w_up, gains, entry, kept, upstream, after):
    _, slots, rows, feats = entry.shape
    ticks, rank = kept.shape[0], w_down.shape[-1]
    width = (ticks + 2) * rank + LANES

    def body(down_ref, up_ref, gain_ref, x_ref, kept_ref, dy_ref, *rest):
        outs, table = rest[:parts], rest[parts]
        for s in range(slots):
            gain = gain_ref[0, s : s + 1, :]
            here = slice(s * rows, (s + 1) * rows)
            streams = [x_ref[0, s].astype(F32)]
            streams += [kept_ref[t, 0, s].astype(F32) for t in range(ticks)]
            scaled = jnp.concatenate([(v * gain).astype(BF16) for v in streams], axis=0)
            latent = dot(scaled, down_ref[0, s]).astype(BF16)
            for i in range(ticks + 1):
                table[here, i * rank : (i + 1) * rank] = latent[i * rows : (i + 1) * rows]
            base = (ticks + 1) * rank
            table[here, base : base + rank] = dot(dy_ref[0, s], up_ref[0, s], NT).astype(BF16)
            squares = on_lanes([squares_of(v) for v in streams], rows)
            table[here, base + rank :] = squares.astype(BF16)
        deal(table, outs)

    return call(
        body,
        [w_down, w_up, gains, entry, kept, upstream],
        [((slots * rows // parts, width), BF16)] * parts,
        "first_partials",
        [pltpu.VMEM((slots * rows, width), BF16)],
        limit=62,
        after=after,
    )


def early_factors(gains, kept, upstream, own, after):
    ticks, _, slots, rows, feats = kept.shape
    half = slots // 2

    def body(gain_ref, kept_ref, dy_ref, own_ref, near, far, own_out):
        own_out[...] = own_ref[...]
        for s in range(slots):
            gain = gain_ref[0, s : s + 1, :]
            out = near if s < half else far
            for t in range(ticks):
                hg = kept_ref[t, 0, s].astype(F32) * gain
                out[s % half, :, t * feats : (t + 1) * feats] = hg.astype(BF16)
            out[s % half, :, ticks * feats :] = dy_ref[0, s]

    return call(
        body,
        [gains, kept, upstream, own],
        [((half, rows, (ticks + 1) * feats), BF16)] * 2 + [(own.shape, own.dtype)],
        "early_factors",
        after=after,
    )


def shared(name, groups, cut, near, far, after=()):
    half, rows, width = near.shape
    count = sum(size for _, size in cut)
    kept = width - count + count // groups

    def body(near_ref, far_ref, *outs):
        mine = group()
        for j in range(2 * half):
            ref = near_ref if j < half else far_ref
            for k, out in enumerate(outs):
                source, target = 0, 0
                for start, size in [*cut, (width, 0)]:
                    plain = start - source
                    if plain:
                        out[j, :, target : target + plain] = ref[j % half, :, source:start]
                    source, target = start, target + plain
                    if size:
                        run = ref[j % half, :, start : start + size].astype(F32)
                        part = lane_part(run, mine ^ k, groups).astype(BF16)
                        out[j, :, target : target + size // groups] = part
                        source, target = start + size, target + size // groups

    return call(
        body, [near, far], [((2 * half, rows, kept), BF16)] * groups, name, after=after
    )


def held_weights(w_down, w_up, after):
    def body(down_ref, up_ref, down_out, up_out, sems):
        copies = [
            pltpu.make_async_copy(down_ref, down_out, sems.at[0]),
            pltpu.make_async_copy(up_ref, up_out, sems.at[1]),
        ]
        for copy in copies:
            copy.start()
        for copy in copies:
            copy.wait()

    return call(
        body,
        [w_down, w_up],
        [(w_down.shape, w_down.dtype), (w_up.shape, w_up.dtype)],
        "held_weights",
        [pltpu.SemaphoreType.DMA((2,))],
        after=after,
        raw=2,
    )


def marker(after):
    def body(out):
        out[...] = jnp.zeros(out.shape, out.dtype)

    return call(body, [], [((8, LANES), F32)], "marker", after=after)


def total(refs):
    value = refs[0][...].astype(F32)
    for ref in refs[1:]:
        value = value + ref[...].astype(F32)
    return value


def scale_of(squares):
    return 1.0 / jnp.sqrt(squares / D + EPS)


def logistic(z):
    return 1.0 / (1.0 + jnp.exp(-z))


def latent_grads(da, u, r):
    z = u * r
    gate = logistic(z)
    dz = da * gate * (1.0 + z * (1.0 - gate))
    dss = (-0.5 / D) * r * r * r * jnp.sum(dz * u, axis=-1, keepdims=True)
    return dz * r, dss


def first_latents(ticks, rank, received, after):
    parts, chunk = len(received), received[0].shape[0]

    def body(*refs):
        ins, (out, held) = refs[:parts], refs[parts:]
        value = total(ins)
        base = (ticks + 2) * rank
        streams = []
        for i in range(ticks + 1):
            u = value[:, i * rank : (i + 1) * rank]
            streams.append((u, scale_of(value[:, base + i : base + i + 1])))
        du, dss = latent_grads(value[:, base - rank : base], *streams[1])
        active = [u * r * logistic(u * r) for u, r in streams]
        out[:, :rank] = active[0].astype(BF16)
        out[:, rank : 2 * rank] = du.astype(BF16)
        out[:, 2 * rank : 2 * rank + LANES] = on_lanes([dss], chunk).astype(BF16)
        for t in range(ticks):
            start = 2 * rank + LANES + t * rank
            out[:, start : start + rank] = active[t + 1].astype(BF16)
        u, r = streams[2]
        held[:, :rank] = u
        held[:, rank:] = on_lanes([r], chunk)

    return call(
        body,
        received,
        [((chunk, (ticks + 2) * rank + LANES), BF16), ((chunk, rank + LANES), F32)],
        "first_latents",
        after=after,
    )


def later_latents(rank, received, held):
    parts, chunk = len(received), received[0].shape[0]

    def body(*refs):
        ins, held, out = refs[:parts], refs[parts], refs[parts + 1]
        value = total(ins)
        z = value[:, :rank] * scale_of(value[:, 2 * rank : 2 * rank + 1])
        grads = value[:, rank : 2 * rank]
        du, dss = latent_grads(grads, held[:, :rank], held[:, rank : rank + 1])
        out[:, :rank] = (z * logistic(z)).astype(BF16)
        out[:, rank : 2 * rank] = du.astype(BF16)
        out[:, 2 * rank :] = on_lanes([dss], chunk).astype(BF16)

    outs = [((chunk, 2 * rank + LANES), BF16)]
    return call(body, [*received, held], outs, "later_latents")[0]


def slot_results(own, x, kept, dy, gain, w_down, w_up):
    rank = w_down.shape[-1]
    y = x.astype(F32) + dot(own[:, :rank], w_up)
    dss = own[:, 2 * rank : 2 * rank + 1].astype(F32)
    dh = dot(own[:, rank : 2 * rank], w_down, NT) * gain
    dh = dh + 2.0 * kept.astype(F32) * dss + dy.astype(F32)
    return y.astype(BF16), dh.astype(BF16)


def middle_results(
    name, mine, received, w_down, w_up, gains, entry, kept, upstream, factors=False, after=()
):
    parts = len(received)
    _, slots, rows, feats = entry.shape
    ticks, rank = kept.shape[0], w_down.shape[-1]
    width = received[0].shape[-1]

    def body(*refs):
        ins, refs = refs[:parts], refs[parts:]
        down_ref, up_ref, gain_ref, x_ref, kept_ref, dy_ref = refs[:6]
        out, table = refs[6], refs[-1]
        collect(ins, table)
        upward = mine()
        for i in range(slots // 2):
            outer, inner = (0, 3)[i], (1, 2)[i]
            s = jnp.where(upward, outer, inner)
            own = table[pl.ds(pl.multiple_of(s * rows, rows), rows), :rank]
            y = x_ref[0, s].astype(F32) + dot(own, up_ref[0, s])
            out[i] = y.astype(BF16)
            s = jnp.where(upward, inner, outer)
            own = table[pl.ds(pl.multiple_of(s * rows, rows), rows), rank : 2 * rank + LANES]
            dh = dot(own[:, :rank], down_ref[0, s], NT) * gain_ref[0, pl.ds(s, 1), :]
            dss = own[:, rank : rank + 1].astype(F32)
            dh = dh + 2.0 * kept_ref[0, 0, s].astype(F32) * dss + dy_ref[0, s].astype(F32)
            out[2 + i] = dh.astype(BF16)
        if factors:
            for s in range(slots):
                own = table[s * rows : (s + 1) * rows, :]
                refs[7][s, :, :rank] = own[:, rank : 2 * rank]
                refs[7][s, :, rank:] = own[:, 2 * rank + LANES :]

    outs = [((slots, rows, feats), BF16)]
    if factors:
        outs.append(((slots, rows, (ticks + 1) * rank), BF16))
    return call(
        body,
        [*received, w_down, w_up, gains, entry, kept, upstream],
        outs,
        name,
        [pltpu.VMEM((slots * rows, width), BF16)],
        after=after,
    )


def later_partials(
    parts, first, second, own, fresh, arriving, w_down, w_up, gains, after
):
    slots, rows, feats = first.shape
    rank = w_down.shape[-1]
    width = 2 * rank + LANES

    def body(*refs):
        a_ref, b_ref, own_ref, fresh_ref, arriving_ref, down_ref, up_ref, gain_ref = refs[:8]
        outs, (x_out, g_out, table) = refs[8 : 8 + parts], refs[8 + parts :]
        odd_one, at_edge = odd(), edge()
        for s in range(slots):
            i, j = s // 2, 2 + s // 2
            ends = (fresh_ref[0, i], own_ref[j]) if s % 2 == 0 else (own_ref[i], arriving_ref[0, i])
            second_x = jnp.where(at_edge, ends[0], b_ref[i])
            second_g = jnp.where(at_edge, ends[1], b_ref[j])
            outer = odd_one if s in (0, 3) else jnp.logical_not(odd_one)
            x = jnp.where(outer, a_ref[i], second_x)
            g = jnp.where(outer, second_g, a_ref[j])
            x_out[s] = x
            g_out[s] = g
            here = slice(s * rows, (s + 1) * rows)
            wide = x.astype(F32)
            scaled = (wide * gain_ref[0, s : s + 1, :]).astype(BF16)
            table[here, :rank] = dot(scaled, down_ref[0, s]).astype(BF16)
            table[here, rank : 2 * rank] = dot(g, up_ref[0, s], NT).astype(BF16)
            table[here, 2 * rank :] = on_lanes([squares_of(wide)], rows).astype(BF16)
        deal(table, outs)

    results = call(
        body,
        [first, second, own, fresh, arriving, w_down, w_up, gains],
        [((slots * rows // parts, width), BF16)] * parts
        + [((slots, rows, feats), BF16)] * 2,
        "later_partials",
        [pltpu.VMEM((slots * rows, width), BF16)],
        after=after,
    )
    return results[:parts], *results[parts:]


def middle_factors(groups, ticks, factors, g, after=()):
    slots, rows, feats = g.shape
    rank = factors.shape[-1] // (ticks + 1)
    some, half = rank // groups, slots // 2

    def body(factor_ref, g_ref, *outs):
        mine = group()
        for s in range(slots):
            for k, out in enumerate(outs[s // half * groups : (s // half + 1) * groups]):
                out[s % half, :, :feats] = g_ref[s]
                out[s % half, :, feats : feats + rank] = factor_ref[s, :, :rank]
                for t in range(ticks):
                    active = factor_ref[s, :, (t + 1) * rank : (t + 2) * rank].astype(F32)
                    part = lane_part(active, mine ^ k, groups).astype(BF16)
                    start = feats + rank + t * some
                    out[s % half, :, start : start + some] = part

    outs = call(
        body,
        [factors, g],
        [((half, rows, feats + rank + ticks * some), BF16)] * (2 * groups),
        "middle_factors",
        after=after,
    )
    return outs[:groups], outs[groups:]


def late_factors(slots, rows, rank, received, after):
    parts, (chunk, width) = len(received), received[0].shape

    def body(*refs):
        ins, (near, far, table) = refs[:parts], refs[parts:]
        here = place()
        for k, ref in enumerate(ins):
            start = pl.multiple_of((here ^ k) * chunk, chunk)
            table[pl.ds(start, chunk), :] = ref[:, rank : 2 * rank]
        for s in range(slots):
            out = near if s < slots // 2 else far
            out[s % (slots // 2)] = table[s * rows : (s + 1) * rows, :]

    return call(
        body,
        received,
        [((slots // 2, rows, rank), BF16)] * 2,
        "late_factors",
        [pltpu.VMEM((slots * rows, rank), BF16)],
        after=after,
    )


def sender(sems):
    copies = []

    def send(source, target):
        copies.append(pltpu.make_async_copy(source, target, sems.at[len(copies)]))
        copies[-1].start()

    def finish():
        for copy in copies:
            copy.wait()

    return send, finish


def last_results(groups, received, w_down, w_up, gains, x, kept, g, early, mid):
    parts, count = len(received), len(early)
    slots, rows, feats = x.shape
    ticks, rank = kept.shape[0], w_down.shape[-1]
    width = received[0].shape[-1]
    half, some = slots // 2, rank // groups

    def body(*refs):
        ins, refs = refs[:parts], refs[parts:]
        down_ref, up_ref, gain_ref, x_ref, kept_ref, g_ref = refs[:6]
        early, mid, refs = refs[6 : 6 + count], refs[6 + count : 6 + 3 * count], refs[6 + 3 * count :]
        y_hbm, dh_hbm, grad_hbm, table, y_out, dh_out, grad_out, sems = refs
        send, finish = sender(sems)
        for j in range(half):
            act, dy = [], []
            for k, e in enumerate(early):
                for i, m in ((j, mid[k]), (half + j, mid[count + k])):
                    start = feats + rank
                    for t in range(ticks):
                        act.append(m[j, :, start + t * some : start + (t + 1) * some])
                    dy += [e[i, :, e.shape[-1] - feats :], m[j, :, :feats]]
            grad_out[j] = dot(jnp.concatenate(act, axis=0), jnp.concatenate(dy, axis=0), TN)
            send(grad_out.at[j], grad_hbm.at[0, j])
        collect(ins, table)
        for s in range(slots):
            y, dh = slot_results(
                table[s * rows : (s + 1) * rows, :],
                x_ref[s],
                kept_ref[ticks - 1, 0, s],
                g_ref[s],
                gain_ref[0, s : s + 1, :],
                down_ref[0, s],
                up_ref[0, s],
            )
            y_out[s] = y
            dh_out[s] = dh
            send(y_out.at[s], y_hbm.at[0, s])
            send(dh_out.at[s], dh_hbm.at[0, s])
        finish()

    return call(
        body,
        [*received, w_down, w_up, gains, x, kept, g, *early, *mid],
        [((1, slots, rows, feats), BF16)] * 2 + [((1, half, some, feats), F32)],
        "last_results",
        [
            pltpu.VMEM((slots * rows, width), BF16),
            pltpu.VMEM((slots, rows, feats), BF16),
            pltpu.VMEM((slots, rows, feats), BF16),
            pltpu.VMEM((half, some, feats), F32),
            pltpu.SemaphoreType.DMA((half + 2 * slots,)),
        ],
        sent=3,
    )


def down_grads(groups, ticks, feats, early, mid, late):
    count, (half, rows, rank) = len(early), late[0].shape
    wide = feats // groups

    def body(*refs):
        early, mid, late = refs[:count], refs[count : 3 * count], refs[3 * count : 5 * count]
        grad_hbm, grad_out, sems = refs[5 * count :]
        send, finish = sender(sems)
        for j in range(half):
            hg, du = [], []
            for k, e in enumerate(early):
                for i, n in ((j, k), (half + j, count + k)):
                    hg += [e[i, :, t * wide : (t + 1) * wide] for t in range(ticks)]
                    du += [mid[n][j, :, feats : feats + rank], late[n][j]]
            grad_out[j] = dot(jnp.concatenate(hg, axis=0), jnp.concatenate(du, axis=0), TN)
            send(grad_out.at[j], grad_hbm.at[0, j])
        finish()

    return call(
        body,
        [*early, *mid, *late],
        [((1, half, wide, rank), F32)],
        "down_grads",
        [pltpu.VMEM((half, wide, rank), F32), pltpu.SemaphoreType.DMA((half,))],
        sent=1,
    )[0]


def per_device(w_down, w_up, gains, entry, kept, upstream, fresh, arriving):
    holders, parts, groups = (lax.axis_size(a) for a in ("pipe", "tensor", "dp"))
    _, slots, rows, feats = entry.shape
    ticks, rank = kept.shape[0], w_down.shape[-1]

    def around(arrays):
        return [arrays[0]] + [
            lax.ppermute(arrays[k], "tensor", [(i, i ^ k) for i in range(parts)])
            for k in range(1, parts)
        ]

    def mirrored(far, k=0):
        pairs = [
            (d * groups + i, (holders - 1 - d) * groups + (i ^ k))
            for d in range(holders)
            for i in range(groups)
        ]
        return lax.ppermute(far, ("pipe", "dp"), pairs)

    def across(arrays):
        return [arrays[0]] + [
            lax.ppermute(arrays[k], "dp", [(i, i ^ k) for i in range(groups)])
            for k in range(1, groups)
        ]

    dealt = first_partials(parts, w_down, w_up, gains, entry, kept, upstream, after=[])
    received = around(dealt)

    near, far, own = early_factors(gains, kept, upstream, dealt[0], after=dealt[1:2])
    far = mirrored(far)

    message, held = first_latents(ticks, rank, [own] + received[1:], after=[near])
    received = around([message] * parts)
    weights = held_weights(w_down, w_up, after=[message])

    tick = (received, *weights, gains, entry, kept, upstream)
    (second,) = middle_results("second_results", odd, *tick)
    swap = [(i, i ^ 1) for i in range(holders)]
    cross = []
    for d in range(holders):
        to = d if d in (0, holders - 1) else d + 1 if d % 2 else d - 1
        for i in range(parts):
            peer = i if to != d else i ^ (parts > 1)
            cross.append((d * parts + i, to * parts + peer))
    from_second = lax.ppermute(second, ("pipe", "tensor"), cross)
    first, factors = middle_results(
        "first_results", even, *tick, factors=True, after=[second] + []
    )
    from_first = lax.ppermute(first, "pipe", swap)

    early = across(
        shared("early_share", groups, [(t * feats, feats) for t in range(ticks)], near, far, [])
    )
    ready = marker(early[1:])

    dealt, x, g = later_partials(
        parts, from_first, from_second, second, fresh, arriving, *weights, gains, after=[]
    )
    received = around(dealt)
    near, far = middle_factors(groups, ticks, factors, g, after=[])
    mid = across(near) + [mirrored(far[k], k) for k in range(groups)]
    message = later_latents(rank, received, held)
    received = around([message] * parts)
    near, far = late_factors(slots, rows, rank, received, after=ready)
    late = across([near] * groups) + [mirrored(far, k) for k in range(groups)]
    y, dh, grad_up = last_results(
        groups, received, *weights, gains, x, kept, g, early, mid
    )
    grad_down = down_grads(groups, ticks, feats, early, mid, late)
    return y, dh, grad_down, grad_up


def solution(mesh):
    return jax.shard_map(
        per_device,
        mesh=mesh,
        in_specs=(
            P("pipe", None, "tensor", None),
            P("pipe", None, None, "tensor"),
            P("pipe", None, "tensor"),
            P("pipe", None, "dp", "tensor"),
            P(None, "pipe", None, "dp", "tensor"),
            P("pipe", None, "dp", "tensor"),
            P(None, None, "dp", "tensor"),
            P(None, None, "dp", "tensor"),
        ),
        out_specs=(
            P("pipe", None, "dp", "tensor"),
            P("pipe", None, "dp", "tensor"),
            P("pipe", None, ("tensor", "dp"), None),
            P("pipe", None, "dp", "tensor"),
        ),
        check_vma=False,
    )
```

```python
import functools

import jax
import jax.numpy as jnp
from jax import lax
from jax.experimental import pallas as pl
from jax.experimental.pallas import tpu as pltpu
from jax.sharding import PartitionSpec as P

D = 5120
EPS = 1e-06
LANES = 128
F32 = jnp.float32
BF16 = jnp.bfloat16

COSTS = {
    "first_partials": 5.0,
    "early_factors": 0.3,
    "held_weights": 0.5,
    "marker": 0.1,
    "first_latents": 4,
    "second_results": 0.8,
    "first_results": 0.8,
    "later_partials": 1.3,
    "middle_factors": 0.1,
    "early_share": 0.3,
    "middle_share": 0.2,
    "late_share": 0.1,
    "later_latents": 3,
    "late_factors": 0.2,
    "last_results": 0.2,
    "up_grads": 0.4,
    "down_grads": 1.5
}
FLOPS_PER_US = 1.1e9

NN = (((1,), (0,)), ((), ()))
NT = (((1,), (1,)), ((), ()))
TN = (((0,), (0,)), ((), ()))


def dot(a, b, dims=NN):
    return lax.dot_general(a, b, dims, preferred_element_type=F32)


def call(body, operands, outs, name, scratch=(), limit=24, after=(), raw=0, sent=0):
    count = len(operands)

    def run(*refs):
        body(*refs[:count], *refs[count + len(after) :])

    return pl.pallas_call(
        run,
        in_specs=[pl.BlockSpec(memory_space=pl.ANY)] * raw
        + [pl.BlockSpec(memory_space=pltpu.VMEM)] * (count - raw)
        + [pl.BlockSpec(memory_space=pl.ANY)] * len(after),
        out_specs=[pl.BlockSpec(memory_space=pl.ANY)] * sent
        + [pl.BlockSpec(memory_space=pltpu.VMEM)] * (len(outs) - sent),
        out_shape=[jax.ShapeDtypeStruct(shape, dtype) for shape, dtype in outs],
        scratch_shapes=list(scratch),
        compiler_params=pltpu.CompilerParams(vmem_limit_bytes=limit * 2**20),
        cost_estimate=pl.CostEstimate(
            flops=round(COSTS[name] * FLOPS_PER_US), bytes_accessed=0, transcendentals=0
        ),
        name=name,
    )(*operands, *after)


def place():
    return lax.axis_index("tensor")


def group():
    return lax.axis_index("dp")


def odd():
    return lax.rem(lax.axis_index("pipe"), 2) == 1


def even():
    return jnp.logical_not(odd())


def edge():
    position = lax.axis_index("pipe")
    return jnp.logical_or(position == 0, position == lax.axis_size("pipe") - 1)


def on_lanes(columns, rows):
    lane = lax.broadcasted_iota(jnp.int32, (rows, LANES), 1)
    out = jnp.zeros((rows, LANES), F32)
    for index, column in enumerate(columns):
        out = jnp.where(lane == index, column, out)
    return out


def squares_of(rows):
    return jnp.sum(rows * rows, axis=-1, keepdims=True)


def lane_part(value, index, count):
    size = value.shape[-1] // count
    out = value[:, :size]
    for i in range(1, count):
        out = jnp.where(index == i, value[:, i * size : (i + 1) * size], out)
    return out


def deal(table, outs):
    here, chunk = place(), outs[0].shape[0]
    for k, out in enumerate(outs):
        start = pl.multiple_of((here ^ k) * chunk, chunk)
        out[...] = table[pl.ds(start, chunk), :]


def collect(ins, table):
    here, chunk = place(), ins[0].shape[0]
    for k, ref in enumerate(ins):
        start = pl.multiple_of((here ^ k) * chunk, chunk)
        table[pl.ds(start, chunk), :] = ref[...]


def first_partials(parts, w_down, w_up, gains, entry, kept, upstream, after):
    _, slots, rows, feats = entry.shape
    ticks, rank = kept.shape[0], w_down.shape[-1]
    width = (ticks + 2) * rank + LANES

    def body(down_ref, up_ref, gain_ref, x_ref, kept_ref, dy_ref, *rest):
        outs, table = rest[:parts], rest[parts]
        for s in range(slots):
            gain = gain_ref[0, s : s + 1, :]
            here = slice(s * rows, (s + 1) * rows)
            streams = [x_ref[0, s].astype(F32)]
            streams += [kept_ref[t, 0, s].astype(F32) for t in range(ticks)]
            scaled = jnp.concatenate([(v * gain).astype(BF16) for v in streams], axis=0)
            latent = dot(scaled, down_ref[0, s]).astype(BF16)
            for i in range(ticks + 1):
                table[here, i * rank : (i + 1) * rank] = latent[i * rows : (i + 1) * rows]
            base = (ticks + 1) * rank
            table[here, base : base + rank] = dot(dy_ref[0, s], up_ref[0, s], NT).astype(BF16)
            squares = on_lanes([squares_of(v) for v in streams], rows)
            table[here, base + rank :] = squares.astype(BF16)
        deal(table, outs)

    return call(
        body,
        [w_down, w_up, gains, entry, kept, upstream],
        [((slots * rows // parts, width), BF16)] * parts,
        "first_partials",
        [pltpu.VMEM((slots * rows, width), BF16)],
        limit=62,
        after=after,
    )


def early_factors(groups, gains, kept, upstream, own, after):
    ticks, _, slots, rows, feats = kept.shape
    half, wide = slots // 2, feats // groups

    def body(gain_ref, kept_ref, dy_ref, own_ref, *outs):
        *near, far, own_out = outs
        own_out[...] = own_ref[...]
        mine = group()
        for s in range(slots):
            gain = gain_ref[0, s : s + 1, :]
            for t in range(ticks):
                hg = kept_ref[t, 0, s].astype(F32) * gain
                if s < half:
                    for k, out in enumerate(near):
                        part = lane_part(hg, mine ^ k, groups).astype(BF16)
                        out[s, :, t * wide : (t + 1) * wide] = part
                else:
                    far[s - half, :, t * feats : (t + 1) * feats] = hg.astype(BF16)
            if s < half:
                for out in near:
                    out[s, :, ticks * wide :] = dy_ref[0, s]
            else:
                far[s - half, :, ticks * feats :] = dy_ref[0, s]

    *near, far, own = call(
        body,
        [gains, kept, upstream, own],
        [((half, rows, ticks * wide + feats), BF16)] * groups
        + [((half, rows, (ticks + 1) * feats), BF16), (own.shape, own.dtype)],
        "early_factors",
        after=after,
    )
    return near, far, own


def early_share(groups, ticks, far, after):
    half, rows, width = far.shape
    feats = width // (ticks + 1)
    wide = feats // groups

    def body(far_ref, *outs):
        mine = group()
        for j in range(half):
            for t in range(ticks):
                hg = far_ref[j, :, t * feats : (t + 1) * feats].astype(F32)
                for k, out in enumerate(outs):
                    part = lane_part(hg, mine ^ k, groups).astype(BF16)
                    out[j, :, t * wide : (t + 1) * wide] = part
            for out in outs:
                out[j, :, ticks * wide :] = far_ref[j, :, ticks * feats :]

    return call(
        body,
        [far],
        [((half, rows, ticks * wide + feats), BF16)] * groups,
        "early_share",
        after=after,
    )


def held_weights(w_down, w_up, after):
    def body(down_ref, up_ref, down_out, up_out, sems):
        copies = [
            pltpu.make_async_copy(down_ref, down_out, sems.at[0]),
            pltpu.make_async_copy(up_ref, up_out, sems.at[1]),
        ]
        for copy in copies:
            copy.start()
        for copy in copies:
            copy.wait()

    return call(
        body,
        [w_down, w_up],
        [(w_down.shape, w_down.dtype), (w_up.shape, w_up.dtype)],
        "held_weights",
        [pltpu.SemaphoreType.DMA((2,))],
        after=after,
        raw=2,
    )


def marker(after):
    def body(out):
        out[...] = jnp.zeros(out.shape, out.dtype)

    return call(body, [], [((8, LANES), F32)], "marker", after=after)


def total(refs):
    value = refs[0][...].astype(F32)
    for ref in refs[1:]:
        value = value + ref[...].astype(F32)
    return value


def scale_of(squares):
    return 1.0 / jnp.sqrt(squares / D + EPS)


def logistic(z):
    return 1.0 / (1.0 + jnp.exp(-z))


def latent_grads(da, u, r):
    z = u * r
    gate = logistic(z)
    dz = da * gate * (1.0 + z * (1.0 - gate))
    dss = (-0.5 / D) * r * r * r * jnp.sum(dz * u, axis=-1, keepdims=True)
    return dz * r, dss


def first_latents(ticks, rank, received, after):
    parts, chunk = len(received), received[0].shape[0]

    def body(*refs):
        ins, (out, held) = refs[:parts], refs[parts:]
        value = total(ins)
        base = (ticks + 2) * rank
        streams = []
        for i in range(ticks + 1):
            u = value[:, i * rank : (i + 1) * rank]
            streams.append((u, scale_of(value[:, base + i : base + i + 1])))
        du, dss = latent_grads(value[:, base - rank : base], *streams[1])
        active = [u * r * logistic(u * r) for u, r in streams]
        out[:, :rank] = active[0].astype(BF16)
        out[:, rank : 2 * rank] = du.astype(BF16)
        out[:, 2 * rank : 2 * rank + LANES] = on_lanes([dss], chunk).astype(BF16)
        for t in range(ticks):
            start = 2 * rank + LANES + t * rank
            out[:, start : start + rank] = active[t + 1].astype(BF16)
        u, r = streams[2]
        held[:, :rank] = u
        held[:, rank:] = on_lanes([r], chunk)

    return call(
        body,
        received,
        [((chunk, (ticks + 2) * rank + LANES), BF16), ((chunk, rank + LANES), F32)],
        "first_latents",
        after=after,
    )


def later_latents(rank, received, held, after):
    parts, chunk = len(received), received[0].shape[0]

    def body(*refs):
        ins, held, out = refs[:parts], refs[parts], refs[parts + 1]
        value = total(ins)
        z = value[:, :rank] * scale_of(value[:, 2 * rank : 2 * rank + 1])
        grads = value[:, rank : 2 * rank]
        du, dss = latent_grads(grads, held[:, :rank], held[:, rank : rank + 1])
        out[:, :rank] = (z * logistic(z)).astype(BF16)
        out[:, rank : 2 * rank] = du.astype(BF16)
        out[:, 2 * rank :] = on_lanes([dss], chunk).astype(BF16)

    outs = [((chunk, 2 * rank + LANES), BF16)]
    return call(body, [*received, held], outs, "later_latents", after=after)[0]


def slot_results(own, x, kept, dy, gain, w_down, w_up):
    rank = w_down.shape[-1]
    y = x.astype(F32) + dot(own[:, :rank], w_up)
    dss = own[:, 2 * rank : 2 * rank + 1].astype(F32)
    dh = dot(own[:, rank : 2 * rank], w_down, NT) * gain
    dh = dh + 2.0 * kept.astype(F32) * dss + dy.astype(F32)
    return y.astype(BF16), dh.astype(BF16)


def middle_results(
    name, mine, received, w_down, w_up, gains, entry, kept, upstream, factors=False, after=()
):
    parts = len(received)
    _, slots, rows, feats = entry.shape
    ticks, rank = kept.shape[0], w_down.shape[-1]
    width = received[0].shape[-1]

    def body(*refs):
        ins, refs = refs[:parts], refs[parts:]
        down_ref, up_ref, gain_ref, x_ref, kept_ref, dy_ref = refs[:6]
        out, table = refs[6], refs[-1]
        collect(ins, table)
        upward = mine()
        for i in range(slots // 2):
            outer, inner = (0, 3)[i], (1, 2)[i]
            s = jnp.where(upward, outer, inner)
            own = table[pl.ds(pl.multiple_of(s * rows, rows), rows), :rank]
            y = x_ref[0, s].astype(F32) + dot(own, up_ref[0, s])
            out[i] = y.astype(BF16)
            s = jnp.where(upward, inner, outer)
            own = table[pl.ds(pl.multiple_of(s * rows, rows), rows), rank : 2 * rank + LANES]
            dh = dot(own[:, :rank], down_ref[0, s], NT) * gain_ref[0, pl.ds(s, 1), :]
            dss = own[:, rank : rank + 1].astype(F32)
            dh = dh + 2.0 * kept_ref[0, 0, s].astype(F32) * dss + dy_ref[0, s].astype(F32)
            out[2 + i] = dh.astype(BF16)
        if factors:
            for s in range(slots):
                own = table[s * rows : (s + 1) * rows, :]
                refs[7][s, :, :rank] = own[:, rank : 2 * rank]
                refs[7][s, :, rank:] = own[:, 2 * rank + LANES :]

    outs = [((slots, rows, feats), BF16)]
    if factors:
        outs.append(((slots, rows, (ticks + 1) * rank), BF16))
    return call(
        body,
        [*received, w_down, w_up, gains, entry, kept, upstream],
        outs,
        name,
        [pltpu.VMEM((slots * rows, width), BF16)],
        after=after,
    )


def later_partials(
    parts, first, second, own, fresh, arriving, w_down, w_up, gains, after
):
    slots, rows, feats = first.shape
    rank = w_down.shape[-1]
    width = 2 * rank + LANES

    def body(*refs):
        a_ref, b_ref, own_ref, fresh_ref, arriving_ref, down_ref, up_ref, gain_ref = refs[:8]
        outs, (x_out, g_out, table) = refs[8 : 8 + parts], refs[8 + parts :]
        odd_one, at_edge = odd(), edge()
        for s in range(slots):
            i, j = s // 2, 2 + s // 2
            ends = (fresh_ref[0, i], own_ref[j]) if s % 2 == 0 else (own_ref[i], arriving_ref[0, i])
            second_x = jnp.where(at_edge, ends[0], b_ref[i])
            second_g = jnp.where(at_edge, ends[1], b_ref[j])
            outer = odd_one if s in (0, 3) else jnp.logical_not(odd_one)
            x = jnp.where(outer, a_ref[i], second_x)
            g = jnp.where(outer, second_g, a_ref[j])
            x_out[s] = x
            g_out[s] = g
            here = slice(s * rows, (s + 1) * rows)
            wide = x.astype(F32)
            scaled = (wide * gain_ref[0, s : s + 1, :]).astype(BF16)
            table[here, :rank] = dot(scaled, down_ref[0, s]).astype(BF16)
            table[here, rank : 2 * rank] = dot(g, up_ref[0, s], NT).astype(BF16)
            table[here, 2 * rank :] = on_lanes([squares_of(wide)], rows).astype(BF16)
        deal(table, outs)

    results = call(
        body,
        [first, second, own, fresh, arriving, w_down, w_up, gains],
        [((slots * rows // parts, width), BF16)] * parts
        + [((slots, rows, feats), BF16)] * 2,
        "later_partials",
        [pltpu.VMEM((slots * rows, width), BF16)],
        after=after,
    )
    return results[:parts], *results[parts:]


def middle_factors(groups, ticks, factors, g, after=()):
    slots, rows, feats = g.shape
    rank = factors.shape[-1] // (ticks + 1)
    some, half = rank // groups, slots // 2

    def body(factor_ref, g_ref, *outs):
        mine = group()
        for s in range(slots):
            for k, out in enumerate(outs[s // half * groups : (s // half + 1) * groups]):
                out[s % half, :, :feats] = g_ref[s]
                out[s % half, :, feats : feats + rank] = factor_ref[s, :, :rank]
                for t in range(ticks):
                    active = factor_ref[s, :, (t + 1) * rank : (t + 2) * rank].astype(F32)
                    part = lane_part(active, mine ^ k, groups).astype(BF16)
                    start = feats + rank + t * some
                    out[s % half, :, start : start + some] = part

    outs = call(
        body,
        [factors, g],
        [((half, rows, feats + rank + ticks * some), BF16)] * (2 * groups),
        "middle_factors",
        after=after,
    )
    return outs[:groups], outs[groups:]


def late_factors(slots, rows, rank, received, after):
    parts, (chunk, width) = len(received), received[0].shape

    def body(*refs):
        ins, (near, far, table) = refs[:parts], refs[parts:]
        here = place()
        for k, ref in enumerate(ins):
            start = pl.multiple_of((here ^ k) * chunk, chunk)
            table[pl.ds(start, chunk), :] = ref[:, rank : 2 * rank]
        for s in range(slots):
            out = near if s < slots // 2 else far
            out[s % (slots // 2)] = table[s * rows : (s + 1) * rows, :]

    return call(
        body,
        received,
        [((slots // 2, rows, rank), BF16)] * 2,
        "late_factors",
        [pltpu.VMEM((slots * rows, rank), BF16)],
        after=after,
    )


def sender(sems):
    copies = []

    def send(source, target):
        copies.append(pltpu.make_async_copy(source, target, sems.at[len(copies)]))
        copies[-1].start()

    def finish():
        for copy in copies:
            copy.wait()

    return send, finish


def last_results(groups, received, w_down, w_up, gains, x, kept, g, early, mid):
    parts, count = len(received), len(early)
    slots, rows, feats = x.shape
    ticks, rank = kept.shape[0], w_down.shape[-1]
    width = received[0].shape[-1]
    half, some = slots // 2, rank // groups

    def body(*refs):
        ins, refs = refs[:parts], refs[parts:]
        down_ref, up_ref, gain_ref, x_ref, kept_ref, g_ref = refs[:6]
        early, mid, refs = refs[6 : 6 + count], refs[6 + count : 6 + 2 * count], refs[6 + 2 * count :]
        y_hbm, dh_hbm, grad_hbm, table, y_out, dh_out, grad_out, sems = refs
        send, finish = sender(sems)
        for j in range(half):
            act, dy = [], []
            for e, m in zip(early, mid):
                start = feats + rank
                for t in range(ticks):
                    act.append(m[j, :, start + t * some : start + (t + 1) * some])
                dy += [e[j, :, e.shape[-1] - feats :], m[j, :, :feats]]
            grad_out[j] = dot(jnp.concatenate(act, axis=0), jnp.concatenate(dy, axis=0), TN)
            send(grad_out.at[j], grad_hbm.at[0, j])
        collect(ins, table)
        for s in range(slots):
            y, dh = slot_results(
                table[s * rows : (s + 1) * rows, :],
                x_ref[s],
                kept_ref[ticks - 1, 0, s],
                g_ref[s],
                gain_ref[0, s : s + 1, :],
                down_ref[0, s],
                up_ref[0, s],
            )
            y_out[s] = y
            dh_out[s] = dh
            send(y_out.at[s], y_hbm.at[0, s])
            send(dh_out.at[s], dh_hbm.at[0, s])
        finish()

    return call(
        body,
        [*received, w_down, w_up, gains, x, kept, g, *early, *mid],
        [((1, slots, rows, feats), BF16)] * 2 + [((1, half, some, feats), F32)],
        "last_results",
        [
            pltpu.VMEM((slots * rows, width), BF16),
            pltpu.VMEM((slots, rows, feats), BF16),
            pltpu.VMEM((slots, rows, feats), BF16),
            pltpu.VMEM((half, some, feats), F32),
            pltpu.SemaphoreType.DMA((half + 2 * slots,)),
        ],
        sent=3,
    )


def down_grads(groups, ticks, feats, early, mid, late):
    count, (half, rows, rank) = len(early), late[0].shape
    wide = feats // groups

    def body(*refs):
        early, mid, late = refs[:count], refs[count : 2 * count], refs[2 * count : 3 * count]
        grad_hbm, grad_out, sems = refs[3 * count :]
        send, finish = sender(sems)
        for j in range(half):
            hg, du = [], []
            for e, m, l in zip(early, mid, late):
                hg += [e[j, :, t * wide : (t + 1) * wide] for t in range(ticks)]
                du += [m[j, :, feats : feats + rank], l[j]]
            grad_out[j] = dot(jnp.concatenate(hg, axis=0), jnp.concatenate(du, axis=0), TN)
            send(grad_out.at[j], grad_hbm.at[0, j])
        finish()

    return call(
        body,
        [*early, *mid, *late],
        [((1, half, wide, rank), F32)],
        "down_grads",
        [pltpu.VMEM((half, wide, rank), F32), pltpu.SemaphoreType.DMA((half,))],
        sent=1,
    )[0]


def per_device(w_down, w_up, gains, entry, kept, upstream, fresh, arriving):
    holders, parts, groups = (lax.axis_size(a) for a in ("pipe", "tensor", "dp"))
    _, slots, rows, feats = entry.shape
    ticks, rank = kept.shape[0], w_down.shape[-1]

    def around(arrays):
        return [arrays[0]] + [
            lax.ppermute(arrays[k], "tensor", [(i, i ^ k) for i in range(parts)])
            for k in range(1, parts)
        ]

    def mirrored(far, k=0):
        pairs = [
            (d * groups + i, (holders - 1 - d) * groups + (i ^ k))
            for d in range(holders)
            for i in range(groups)
        ]
        return lax.ppermute(far, ("pipe", "dp"), pairs)

    def across(arrays):
        return [arrays[0]] + [
            lax.ppermute(arrays[k], "dp", [(i, i ^ k) for i in range(groups)])
            for k in range(1, groups)
        ]

    dealt = first_partials(parts, w_down, w_up, gains, entry, kept, upstream, after=[])
    received = around(dealt)

    near, far, own = early_factors(groups, gains, kept, upstream, dealt[0], after=dealt[1:2])
    early = across(near)
    far = mirrored(far)

    message, held = first_latents(ticks, rank, [own] + received[1:], after=[own])
    received = around([message] * parts)
    weights = held_weights(w_down, w_up, after=[message])

    tick = (received, *weights, gains, entry, kept, upstream)
    (second,) = middle_results("second_results", odd, *tick)
    swap = [(i, i ^ 1) for i in range(holders)]
    cross = []
    for d in range(holders):
        to = d if d in (0, holders - 1) else d + 1 if d % 2 else d - 1
        for i in range(parts):
            peer = i if to != d else i ^ (parts > 1)
            cross.append((d * parts + i, to * parts + peer))
    from_second = lax.ppermute(second, ("pipe", "tensor"), cross)
    first, factors = middle_results(
        "first_results", even, *tick, factors=True, after=[second] + []
    )
    from_first = lax.ppermute(first, "pipe", swap)

    early += across(early_share(groups, ticks, far, after=[second]))
    ready_near = marker(early[1:groups])
    ready = marker(early[groups + 1 :])

    dealt, x, g = later_partials(
        parts, from_first, from_second, second, fresh, arriving, *weights, gains, after=ready_near
    )
    received = around(dealt)
    near, far = middle_factors(groups, ticks, factors, g, after=[])
    mid = across(near) + [mirrored(far[k], k) for k in range(groups)]
    message = later_latents(rank, received, held, after=ready)
    received = around([message] * parts)
    near, far = late_factors(slots, rows, rank, received, after=[])
    late = across([near] * groups) + [mirrored(far, k) for k in range(groups)]
    y, dh, grad_up = last_results(
        groups, received, *weights, gains, x, kept, g, early, mid
    )
    grad_down = down_grads(groups, ticks, feats, early, mid, late)
    return y, dh, grad_down, grad_up


def solution(mesh):
    return jax.shard_map(
        per_device,
        mesh=mesh,
        in_specs=(
            P("pipe", None, "tensor", None),
            P("pipe", None, None, "tensor"),
            P("pipe", None, "tensor"),
            P("pipe", None, "dp", "tensor"),
            P(None, "pipe", None, "dp", "tensor"),
            P("pipe", None, "dp", "tensor"),
            P(None, None, "dp", "tensor"),
            P(None, None, "dp", "tensor"),
        ),
        out_specs=(
            P("pipe", None, "dp", "tensor"),
            P("pipe", None, "dp", "tensor"),
            P("pipe", None, ("tensor", "dp"), None),
            P("pipe", None, "dp", "tensor"),
        ),
        check_vma=False,
    )
```

```python
import functools

import jax
import jax.numpy as jnp
from jax import lax
from jax.experimental import pallas as pl
from jax.experimental.pallas import tpu as pltpu
from jax.sharding import PartitionSpec as P

D = 5120
EPS = 1e-06
LANES = 128
F32 = jnp.float32
BF16 = jnp.bfloat16

COSTS = {
    "first_partials": 5.0,
    "early_factors": 0.3,
    "held_weights": 0.5,
    "near_ready": 1,
    "far_ready": 0.1,
    "first_latents": 4,
    "second_results": 0.8,
    "first_results": 0.8,
    "later_partials": 1.3,
    "middle_factors": 0.1,
    "early_share": 0.3,
    "middle_share": 0.2,
    "late_share": 0.1,
    "later_latents": 3,
    "late_factors": 0.2,
    "last_results": 0.2,
    "up_grads": 0.4,
    "down_grads": 1.5
}
FLOPS_PER_US = 1.1e9

NN = (((1,), (0,)), ((), ()))
NT = (((1,), (1,)), ((), ()))
TN = (((0,), (0,)), ((), ()))


def dot(a, b, dims=NN):
    return lax.dot_general(a, b, dims, preferred_element_type=F32)


def call(body, operands, outs, name, scratch=(), limit=24, after=(), raw=0, sent=0):
    count = len(operands)

    def run(*refs):
        body(*refs[:count], *refs[count + len(after) :])

    return pl.pallas_call(
        run,
        in_specs=[pl.BlockSpec(memory_space=pl.ANY)] * raw
        + [pl.BlockSpec(memory_space=pltpu.VMEM)] * (count - raw)
        + [pl.BlockSpec(memory_space=pl.ANY)] * len(after),
        out_specs=[pl.BlockSpec(memory_space=pl.ANY)] * sent
        + [pl.BlockSpec(memory_space=pltpu.VMEM)] * (len(outs) - sent),
        out_shape=[jax.ShapeDtypeStruct(shape, dtype) for shape, dtype in outs],
        scratch_shapes=list(scratch),
        compiler_params=pltpu.CompilerParams(vmem_limit_bytes=limit * 2**20),
        cost_estimate=pl.CostEstimate(
            flops=round(COSTS[name] * FLOPS_PER_US), bytes_accessed=0, transcendentals=0
        ),
        name=name,
    )(*operands, *after)


def place():
    return lax.axis_index("tensor")


def group():
    return lax.axis_index("dp")


def odd():
    return lax.rem(lax.axis_index("pipe"), 2) == 1


def even():
    return jnp.logical_not(odd())


def edge():
    position = lax.axis_index("pipe")
    return jnp.logical_or(position == 0, position == lax.axis_size("pipe") - 1)


def on_lanes(columns, rows):
    lane = lax.broadcasted_iota(jnp.int32, (rows, LANES), 1)
    out = jnp.zeros((rows, LANES), F32)
    for index, column in enumerate(columns):
        out = jnp.where(lane == index, column, out)
    return out


def squares_of(rows):
    return jnp.sum(rows * rows, axis=-1, keepdims=True)


def lane_part(value, index, count):
    size = value.shape[-1] // count
    out = value[:, :size]
    for i in range(1, count):
        out = jnp.where(index == i, value[:, i * size : (i + 1) * size], out)
    return out


def deal(table, outs):
    here, chunk = place(), outs[0].shape[0]
    for k, out in enumerate(outs):
        start = pl.multiple_of((here ^ k) * chunk, chunk)
        out[...] = table[pl.ds(start, chunk), :]


def collect(ins, table):
    here, chunk = place(), ins[0].shape[0]
    for k, ref in enumerate(ins):
        start = pl.multiple_of((here ^ k) * chunk, chunk)
        table[pl.ds(start, chunk), :] = ref[...]


def first_partials(parts, w_down, w_up, gains, entry, kept, upstream, after):
    _, slots, rows, feats = entry.shape
    ticks, rank = kept.shape[0], w_down.shape[-1]
    width = (ticks + 2) * rank + LANES

    def body(down_ref, up_ref, gain_ref, x_ref, kept_ref, dy_ref, *rest):
        outs, table = rest[:parts], rest[parts]
        for s in range(slots):
            gain = gain_ref[0, s : s + 1, :]
            here = slice(s * rows, (s + 1) * rows)
            streams = [x_ref[0, s].astype(F32)]
            streams += [kept_ref[t, 0, s].astype(F32) for t in range(ticks)]
            scaled = jnp.concatenate([(v * gain).astype(BF16) for v in streams], axis=0)
            latent = dot(scaled, down_ref[0, s]).astype(BF16)
            for i in range(ticks + 1):
                table[here, i * rank : (i + 1) * rank] = latent[i * rows : (i + 1) * rows]
            base = (ticks + 1) * rank
            table[here, base : base + rank] = dot(dy_ref[0, s], up_ref[0, s], NT).astype(BF16)
            squares = on_lanes([squares_of(v) for v in streams], rows)
            table[here, base + rank :] = squares.astype(BF16)
        deal(table, outs)

    return call(
        body,
        [w_down, w_up, gains, entry, kept, upstream],
        [((slots * rows // parts, width), BF16)] * parts,
        "first_partials",
        [pltpu.VMEM((slots * rows, width), BF16)],
        limit=62,
        after=after,
    )


def early_factors(groups, gains, kept, upstream, own, after):
    ticks, _, slots, rows, feats = kept.shape
    half, wide = slots // 2, feats // groups

    def body(gain_ref, kept_ref, dy_ref, own_ref, *outs):
        *near, far, own_out = outs
        own_out[...] = own_ref[...]
        mine = group()
        for s in range(slots):
            gain = gain_ref[0, s : s + 1, :]
            for t in range(ticks):
                hg = kept_ref[t, 0, s].astype(F32) * gain
                if s < half:
                    for k, out in enumerate(near):
                        part = lane_part(hg, mine ^ k, groups).astype(BF16)
                        out[s, :, t * wide : (t + 1) * wide] = part
                else:
                    far[s - half, :, t * feats : (t + 1) * feats] = hg.astype(BF16)
            if s < half:
                for out in near:
                    out[s, :, ticks * wide :] = dy_ref[0, s]
            else:
                far[s - half, :, ticks * feats :] = dy_ref[0, s]

    *near, far, own = call(
        body,
        [gains, kept, upstream, own],
        [((half, rows, ticks * wide + feats), BF16)] * groups
        + [((half, rows, (ticks + 1) * feats), BF16), (own.shape, own.dtype)],
        "early_factors",
        after=after,
    )
    return near, far, own


def early_share(groups, ticks, far, after):
    half, rows, width = far.shape
    feats = width // (ticks + 1)
    wide = feats // groups

    def body(far_ref, *outs):
        mine = group()
        for j in range(half):
            for t in range(ticks):
                hg = far_ref[j, :, t * feats : (t + 1) * feats].astype(F32)
                for k, out in enumerate(outs):
                    part = lane_part(hg, mine ^ k, groups).astype(BF16)
                    out[j, :, t * wide : (t + 1) * wide] = part
            for out in outs:
                out[j, :, ticks * wide :] = far_ref[j, :, ticks * feats :]

    return call(
        body,
        [far],
        [((half, rows, ticks * wide + feats), BF16)] * groups,
        "early_share",
        after=after,
    )


def held_weights(w_down, w_up, after):
    def body(down_ref, up_ref, down_out, up_out, sems):
        copies = [
            pltpu.make_async_copy(down_ref, down_out, sems.at[0]),
            pltpu.make_async_copy(up_ref, up_out, sems.at[1]),
        ]
        for copy in copies:
            copy.start()
        for copy in copies:
            copy.wait()

    return call(
        body,
        [w_down, w_up],
        [(w_down.shape, w_down.dtype), (w_up.shape, w_up.dtype)],
        "held_weights",
        [pltpu.SemaphoreType.DMA((2,))],
        after=after,
        raw=2,
    )


def marker(name, after):
    def body(out):
        out[...] = jnp.zeros(out.shape, out.dtype)

    return call(body, [], [((8, LANES), F32)], name, after=after)


def total(refs):
    value = refs[0][...].astype(F32)
    for ref in refs[1:]:
        value = value + ref[...].astype(F32)
    return value


def scale_of(squares):
    return 1.0 / jnp.sqrt(squares / D + EPS)


def logistic(z):
    return 1.0 / (1.0 + jnp.exp(-z))


def latent_grads(da, u, r):
    z = u * r
    gate = logistic(z)
    dz = da * gate * (1.0 + z * (1.0 - gate))
    dss = (-0.5 / D) * r * r * r * jnp.sum(dz * u, axis=-1, keepdims=True)
    return dz * r, dss


def first_latents(ticks, rank, received, after):
    parts, chunk = len(received), received[0].shape[0]

    def body(*refs):
        ins, (out, held) = refs[:parts], refs[parts:]
        value = total(ins)
        base = (ticks + 2) * rank
        streams = []
        for i in range(ticks + 1):
            u = value[:, i * rank : (i + 1) * rank]
            streams.append((u, scale_of(value[:, base + i : base + i + 1])))
        du, dss = latent_grads(value[:, base - rank : base], *streams[1])
        active = [u * r * logistic(u * r) for u, r in streams]
        out[:, :rank] = active[0].astype(BF16)
        out[:, rank : 2 * rank] = du.astype(BF16)
        out[:, 2 * rank : 2 * rank + LANES] = on_lanes([dss], chunk).astype(BF16)
        for t in range(ticks):
            start = 2 * rank + LANES + t * rank
            out[:, start : start + rank] = active[t + 1].astype(BF16)
        u, r = streams[2]
        held[:, :rank] = u
        held[:, rank:] = on_lanes([r], chunk)

    return call(
        body,
        received,
        [((chunk, (ticks + 2) * rank + LANES), BF16), ((chunk, rank + LANES), F32)],
        "first_latents",
        after=after,
    )


def later_latents(rank, received, held, after):
    parts, chunk = len(received), received[0].shape[0]

    def body(*refs):
        ins, held, out = refs[:parts], refs[parts], refs[parts + 1]
        value = total(ins)
        z = value[:, :rank] * scale_of(value[:, 2 * rank : 2 * rank + 1])
        grads = value[:, rank : 2 * rank]
        du, dss = latent_grads(grads, held[:, :rank], held[:, rank : rank + 1])
        out[:, :rank] = (z * logistic(z)).astype(BF16)
        out[:, rank : 2 * rank] = du.astype(BF16)
        out[:, 2 * rank :] = on_lanes([dss], chunk).astype(BF16)

    outs = [((chunk, 2 * rank + LANES), BF16)]
    return call(body, [*received, held], outs, "later_latents", after=after)[0]


def slot_results(own, x, kept, dy, gain, w_down, w_up):
    rank = w_down.shape[-1]
    y = x.astype(F32) + dot(own[:, :rank], w_up)
    dss = own[:, 2 * rank : 2 * rank + 1].astype(F32)
    dh = dot(own[:, rank : 2 * rank], w_down, NT) * gain
    dh = dh + 2.0 * kept.astype(F32) * dss + dy.astype(F32)
    return y.astype(BF16), dh.astype(BF16)


def middle_results(
    name, mine, received, w_down, w_up, gains, entry, kept, upstream, factors=False, after=()
):
    parts = len(received)
    _, slots, rows, feats = entry.shape
    ticks, rank = kept.shape[0], w_down.shape[-1]
    width = received[0].shape[-1]

    def body(*refs):
        ins, refs = refs[:parts], refs[parts:]
        down_ref, up_ref, gain_ref, x_ref, kept_ref, dy_ref = refs[:6]
        out, table = refs[6], refs[-1]
        collect(ins, table)
        upward = mine()
        for i in range(slots // 2):
            outer, inner = (0, 3)[i], (1, 2)[i]
            s = jnp.where(upward, outer, inner)
            own = table[pl.ds(pl.multiple_of(s * rows, rows), rows), :rank]
            y = x_ref[0, s].astype(F32) + dot(own, up_ref[0, s])
            out[i] = y.astype(BF16)
            s = jnp.where(upward, inner, outer)
            own = table[pl.ds(pl.multiple_of(s * rows, rows), rows), rank : 2 * rank + LANES]
            dh = dot(own[:, :rank], down_ref[0, s], NT) * gain_ref[0, pl.ds(s, 1), :]
            dss = own[:, rank : rank + 1].astype(F32)
            dh = dh + 2.0 * kept_ref[0, 0, s].astype(F32) * dss + dy_ref[0, s].astype(F32)
            out[2 + i] = dh.astype(BF16)
        if factors:
            for s in range(slots):
                own = table[s * rows : (s + 1) * rows, :]
                refs[7][s, :, :rank] = own[:, rank : 2 * rank]
                refs[7][s, :, rank:] = own[:, 2 * rank + LANES :]

    outs = [((slots, rows, feats), BF16)]
    if factors:
        outs.append(((slots, rows, (ticks + 1) * rank), BF16))
    return call(
        body,
        [*received, w_down, w_up, gains, entry, kept, upstream],
        outs,
        name,
        [pltpu.VMEM((slots * rows, width), BF16)],
        after=after,
    )


def later_partials(
    parts, first, second, own, fresh, arriving, w_down, w_up, gains, after
):
    slots, rows, feats = first.shape
    rank = w_down.shape[-1]
    width = 2 * rank + LANES

    def body(*refs):
        a_ref, b_ref, own_ref, fresh_ref, arriving_ref, down_ref, up_ref, gain_ref = refs[:8]
        outs, (x_out, g_out, table) = refs[8 : 8 + parts], refs[8 + parts :]
        odd_one, at_edge = odd(), edge()
        for s in range(slots):
            i, j = s // 2, 2 + s // 2
            ends = (fresh_ref[0, i], own_ref[j]) if s % 2 == 0 else (own_ref[i], arriving_ref[0, i])
            second_x = jnp.where(at_edge, ends[0], b_ref[i])
            second_g = jnp.where(at_edge, ends[1], b_ref[j])
            outer = odd_one if s in (0, 3) else jnp.logical_not(odd_one)
            x = jnp.where(outer, a_ref[i], second_x)
            g = jnp.where(outer, second_g, a_ref[j])
            x_out[s] = x
            g_out[s] = g
            here = slice(s * rows, (s + 1) * rows)
            wide = x.astype(F32)
            scaled = (wide * gain_ref[0, s : s + 1, :]).astype(BF16)
            table[here, :rank] = dot(scaled, down_ref[0, s]).astype(BF16)
            table[here, rank : 2 * rank] = dot(g, up_ref[0, s], NT).astype(BF16)
            table[here, 2 * rank :] = on_lanes([squares_of(wide)], rows).astype(BF16)
        deal(table, outs)

    results = call(
        body,
        [first, second, own, fresh, arriving, w_down, w_up, gains],
        [((slots * rows // parts, width), BF16)] * parts
        + [((slots, rows, feats), BF16)] * 2,
        "later_partials",
        [pltpu.VMEM((slots * rows, width), BF16)],
        after=after,
    )
    return results[:parts], *results[parts:]


def middle_factors(groups, ticks, factors, g, after=()):
    slots, rows, feats = g.shape
    rank = factors.shape[-1] // (ticks + 1)
    some, half = rank // groups, slots // 2

    def body(factor_ref, g_ref, *outs):
        mine = group()
        for s in range(slots):
            for k, out in enumerate(outs[s // half * groups : (s // half + 1) * groups]):
                out[s % half, :, :feats] = g_ref[s]
                out[s % half, :, feats : feats + rank] = factor_ref[s, :, :rank]
                for t in range(ticks):
                    active = factor_ref[s, :, (t + 1) * rank : (t + 2) * rank].astype(F32)
                    part = lane_part(active, mine ^ k, groups).astype(BF16)
                    start = feats + rank + t * some
                    out[s % half, :, start : start + some] = part

    outs = call(
        body,
        [factors, g],
        [((half, rows, feats + rank + ticks * some), BF16)] * (2 * groups),
        "middle_factors",
        after=after,
    )
    return outs[:groups], outs[groups:]


def late_factors(slots, rows, rank, received, after):
    parts, (chunk, width) = len(received), received[0].shape

    def body(*refs):
        ins, (near, far, table) = refs[:parts], refs[parts:]
        here = place()
        for k, ref in enumerate(ins):
            start = pl.multiple_of((here ^ k) * chunk, chunk)
            table[pl.ds(start, chunk), :] = ref[:, rank : 2 * rank]
        for s in range(slots):
            out = near if s < slots // 2 else far
            out[s % (slots // 2)] = table[s * rows : (s + 1) * rows, :]

    return call(
        body,
        received,
        [((slots // 2, rows, rank), BF16)] * 2,
        "late_factors",
        [pltpu.VMEM((slots * rows, rank), BF16)],
        after=after,
    )


def sender(sems):
    copies = []

    def send(source, target):
        copies.append(pltpu.make_async_copy(source, target, sems.at[len(copies)]))
        copies[-1].start()

    def finish():
        for copy in copies:
            copy.wait()

    return send, finish


def last_results(groups, received, w_down, w_up, gains, x, kept, g, early, mid):
    parts, count = len(received), len(early)
    slots, rows, feats = x.shape
    ticks, rank = kept.shape[0], w_down.shape[-1]
    width = received[0].shape[-1]
    half, some = slots // 2, rank // groups

    def body(*refs):
        ins, refs = refs[:parts], refs[parts:]
        down_ref, up_ref, gain_ref, x_ref, kept_ref, g_ref = refs[:6]
        early, mid, refs = refs[6 : 6 + count], refs[6 + count : 6 + 2 * count], refs[6 + 2 * count :]
        y_hbm, dh_hbm, grad_hbm, table, y_out, dh_out, grad_out, sems = refs
        send, finish = sender(sems)
        for j in range(half):
            act, dy = [], []
            for e, m in zip(early, mid):
                start = feats + rank
                for t in range(ticks):
                    act.append(m[j, :, start + t * some : start + (t + 1) * some])
                dy += [e[j, :, e.shape[-1] - feats :], m[j, :, :feats]]
            grad_out[j] = dot(jnp.concatenate(act, axis=0), jnp.concatenate(dy, axis=0), TN)
            send(grad_out.at[j], grad_hbm.at[0, j])
        collect(ins, table)
        for s in range(slots):
            y, dh = slot_results(
                table[s * rows : (s + 1) * rows, :],
                x_ref[s],
                kept_ref[ticks - 1, 0, s],
                g_ref[s],
                gain_ref[0, s : s + 1, :],
                down_ref[0, s],
                up_ref[0, s],
            )
            y_out[s] = y
            dh_out[s] = dh
            send(y_out.at[s], y_hbm.at[0, s])
            send(dh_out.at[s], dh_hbm.at[0, s])
        finish()

    return call(
        body,
        [*received, w_down, w_up, gains, x, kept, g, *early, *mid],
        [((1, slots, rows, feats), BF16)] * 2 + [((1, half, some, feats), F32)],
        "last_results",
        [
            pltpu.VMEM((slots * rows, width), BF16),
            pltpu.VMEM((slots, rows, feats), BF16),
            pltpu.VMEM((slots, rows, feats), BF16),
            pltpu.VMEM((half, some, feats), F32),
            pltpu.SemaphoreType.DMA((half + 2 * slots,)),
        ],
        sent=3,
    )


def down_grads(groups, ticks, feats, early, mid, late):
    count, (half, rows, rank) = len(early), late[0].shape
    wide = feats // groups

    def body(*refs):
        early, mid, late = refs[:count], refs[count : 2 * count], refs[2 * count : 3 * count]
        grad_hbm, grad_out, sems = refs[3 * count :]
        send, finish = sender(sems)
        for j in range(half):
            hg, du = [], []
            for e, m, l in zip(early, mid, late):
                hg += [e[j, :, t * wide : (t + 1) * wide] for t in range(ticks)]
                du += [m[j, :, feats : feats + rank], l[j]]
            grad_out[j] = dot(jnp.concatenate(hg, axis=0), jnp.concatenate(du, axis=0), TN)
            send(grad_out.at[j], grad_hbm.at[0, j])
        finish()

    return call(
        body,
        [*early, *mid, *late],
        [((1, half, wide, rank), F32)],
        "down_grads",
        [pltpu.VMEM((half, wide, rank), F32), pltpu.SemaphoreType.DMA((half,))],
        sent=1,
    )[0]


def per_device(w_down, w_up, gains, entry, kept, upstream, fresh, arriving):
    holders, parts, groups = (lax.axis_size(a) for a in ("pipe", "tensor", "dp"))
    _, slots, rows, feats = entry.shape
    ticks, rank = kept.shape[0], w_down.shape[-1]

    def around(arrays):
        return [arrays[0]] + [
            lax.ppermute(arrays[k], "tensor", [(i, i ^ k) for i in range(parts)])
            for k in range(1, parts)
        ]

    def mirrored(far, k=0):
        pairs = [
            (d * groups + i, (holders - 1 - d) * groups + (i ^ k))
            for d in range(holders)
            for i in range(groups)
        ]
        return lax.ppermute(far, ("pipe", "dp"), pairs)

    def across(arrays):
        return [arrays[0]] + [
            lax.ppermute(arrays[k], "dp", [(i, i ^ k) for i in range(groups)])
            for k in range(1, groups)
        ]

    dealt = first_partials(parts, w_down, w_up, gains, entry, kept, upstream, after=[])
    received = around(dealt)

    near, far, own = early_factors(groups, gains, kept, upstream, dealt[0], after=dealt[1:2])
    early = across(near)
    far = mirrored(far)

    message, held = first_latents(ticks, rank, [own] + received[1:], after=[own])
    received = around([message] * parts)
    weights = held_weights(w_down, w_up, after=[message])

    tick = (received, *weights, gains, entry, kept, upstream)
    (second,) = middle_results("second_results", odd, *tick)
    swap = [(i, i ^ 1) for i in range(holders)]
    cross = []
    for d in range(holders):
        to = d if d in (0, holders - 1) else d + 1 if d % 2 else d - 1
        for i in range(parts):
            peer = i if to != d else i ^ (parts > 1)
            cross.append((d * parts + i, to * parts + peer))
    from_second = lax.ppermute(second, ("pipe", "tensor"), cross)
    first, factors = middle_results(
        "first_results", even, *tick, factors=True, after=[second] + []
    )
    from_first = lax.ppermute(first, "pipe", swap)

    early += across(early_share(groups, ticks, far, after=[second]))
    ready_near = marker("near_ready", [*early[1:groups], from_second])
    ready = marker("far_ready", early[groups + 1 :])

    dealt, x, g = later_partials(
        parts, from_first, from_second, second, fresh, arriving, *weights, gains, after=ready_near
    )
    received = around(dealt)
    near, far = middle_factors(groups, ticks, factors, g, after=[])
    mid = across(near) + [mirrored(far[k], k) for k in range(groups)]
    message = later_latents(rank, received, held, after=ready)
    received = around([message] * parts)
    near, far = late_factors(slots, rows, rank, received, after=[])
    late = across([near] * groups) + [mirrored(far, k) for k in range(groups)]
    y, dh, grad_up = last_results(
        groups, received, *weights, gains, x, kept, g, early, mid
    )
    grad_down = down_grads(groups, ticks, feats, early, mid, late)
    return y, dh, grad_down, grad_up


def solution(mesh):
    return jax.shard_map(
        per_device,
        mesh=mesh,
        in_specs=(
            P("pipe", None, "tensor", None),
            P("pipe", None, None, "tensor"),
            P("pipe", None, "tensor"),
            P("pipe", None, "dp", "tensor"),
            P(None, "pipe", None, "dp", "tensor"),
            P("pipe", None, "dp", "tensor"),
            P(None, None, "dp", "tensor"),
            P(None, None, "dp", "tensor"),
        ),
        out_specs=(
            P("pipe", None, "dp", "tensor"),
            P("pipe", None, "dp", "tensor"),
            P("pipe", None, ("tensor", "dp"), None),
            P("pipe", None, "dp", "tensor"),
        ),
        check_vma=False,
    )
```
